32 devices in a mesh: dp: 8 (over z, core), tensor: 4 (over y, x).
Axes of the slice: x: 2, y: 2, z: 4, core: 2. Of those that a mesh axis runs over, the one named last changes fastest.
Arguments:
- tokens: bfloat16 [2, 8192, 2560], P(None, ('dp', 'tensor')), may hold values from -6 to 6
- prefix: int32 [2, 8], P(None, 'dp'), may hold values from 102 to 512
- input_gain: bfloat16 [2560], P(('dp', 'tensor')), may hold values from 0.5 to 1.5
- query_down: bfloat16 [2560, 768], P(('dp', 'tensor')), may hold values from -0.125 to 0.125
- query_gain: bfloat16 [768], P(('dp', 'tensor')), may hold values from 0.5 to 1.5
- query_up: bfloat16 [768, 3840], P('dp', 'tensor'), may hold values from -0.21875 to 0.21875
- latent_down: bfloat16 [2560, 288], P(('dp', 'tensor')), may hold values from -0.125 to 0.125
- latent_gain: bfloat16 [256], P(('dp', 'tensor')), may hold values from 0.5 to 1.5
- latent_up: bfloat16 [256, 5120], P('dp', 'tensor'), may hold values from -0.375 to 0.375
- out_proj: bfloat16 [2560, 2560], P('tensor', 'dp'), may hold values from -4 to 4
- post_gain: bfloat16 [2560], P(('dp', 'tensor')), may hold values from 0.5 to 1.5
- gate_proj: bfloat16 [2560, 6400], P('dp', 'tensor'), may hold values from -0.125 to 0.125
- up_proj: bfloat16 [2560, 6400], P('dp', 'tensor'), may hold values from -0.125 to 0.125
- down_proj: bfloat16 [6400, 2560], P('tensor', 'dp'), may hold values from -0.875 to 0.875
- cotangent: bfloat16 [2, 8192, 2560], P(None, ('dp', 'tensor')), may hold values from -6 to 6
Outputs:
- mixed: bfloat16 [2, 8192, 2560], P(None, ('dp', 'tensor'))
- d_tokens: float32 [2, 8192, 2560], P(None, ('dp', 'tensor'))
- input_gain_grad: float32 [2560], P(('dp', 'tensor'))
- query_down_grad: float32 [2560, 768], P(('dp', 'tensor'))
- query_gain_grad: float32 [768], P(('dp', 'tensor'))
- query_up_grad: float32 [768, 3840], P('dp', 'tensor')
- latent_down_grad: float32 [2560, 288], P(('dp', 'tensor'))
- latent_gain_grad: float32 [256], P(('dp', 'tensor'))
- latent_up_grad: float32 [256, 5120], P('dp', 'tensor')
- out_proj_grad: float32 [2560, 2560], P('tensor', 'dp')
- post_gain_grad: float32 [2560], P(('dp', 'tensor'))
- gate_grad: float32 [2560, 6400], P('dp', 'tensor')
- up_grad: float32 [2560, 6400], P('dp', 'tensor')
- down_grad: float32 [6400, 2560], P('tensor', 'dp')
The draws below stay inside these ranges and needn't reach their ends.
Inputs may be any that keep to these rules, and one draw needn't show every extreme that they name: prefix of each sequence: its first that many tokens attend to each other both ways.
All inputs are finite; a program needn't handle non-finite values.
Results may differ from the reference program's by a relative error of at most 0.024.
Values may be sent and summed in bfloat16 or wider, within the bound.
No kernel may reach another device: no remote copies, remote signals or barrier semaphores. Data moves between devices by JAX's collectives and lax.ppermute only.
A program may use at most 208 MiB of HBM per device.

```python
import math
import jax
import jax.numpy as jnp
from jax import lax

D = 2560
H = 40
NOPE = 64
ROPE = 32
VD = 64
QR = 768
KVR = 256
FF = 6400
SEQ_LEN = 1024
MB = 2
N_DP = 8


def place_ends(entries, key, low, largest):
    shape = entries.shape
    index_at = [jax.random.randint(jax.random.fold_in(key, axis), (), 0, shape[axis]) for axis in range(len(shape))]
    entries = entries.at[tuple(index_at)].set(low)
    longest = shape.index(max(shape))
    index_at[longest] = (index_at[longest] + 1) % shape[longest]
    return entries.at[tuple(index_at)].set(largest)


def level_of(own_key, shape, shards, least, top_value):
    gain, own = 1.0, jax.random.fold_in(own_key, 6)
    for axis_at, blocks in shards:
        draws = jnp.exp(jax.random.uniform(jax.random.fold_in(own, axis_at), (blocks,), jnp.float32, least / len(shards), top_value / len(shards)))
        gain = gain * jnp.repeat(draws, shape[axis_at] // blocks).reshape([-1 if axis == axis_at else 1 for axis in range(len(shape))])
    return gain


def noise(stream_key, dims, scale, limit, split=(), dtype=jnp.bfloat16):
    entries = scale * jax.random.normal(stream_key, dims, jnp.float32)
    if split:
        entries = entries * level_of(stream_key, dims, split, -0.22, 0.18)
    return jnp.clip(entries, -limit, limit).astype(dtype)


def setup_inputs(seed: int = 0) -> dict:
    keys = jax.random.split(jax.random.key(seed), 16)
    tokens = noise(keys[0], (MB, N_DP * SEQ_LEN, D), 1.0, 6.0, ((1, 32),))
    prefix = place_ends(jax.random.randint(keys[1], (MB, N_DP), SEQ_LEN // 10, SEQ_LEN // 2 + 1), jax.random.fold_in(keys[1], 1), SEQ_LEN // 10, (SEQ_LEN // 2 + 1) - 1).astype(jnp.int32)
    input_gain = jnp.clip(1.0 + 0.1 * jax.random.normal(keys[2], (D,), jnp.float32), 0.5, 1.5).astype(jnp.bfloat16)
    query_down = noise(keys[3], (D, QR), D ** -0.5, 0.125, ((0, 32),))
    query_gain = jnp.clip(1.0 + 0.1 * jax.random.normal(keys[4], (QR,), jnp.float32), 0.5, 1.5).astype(jnp.bfloat16)
    query_up = noise(keys[5], (QR, H * (NOPE + ROPE)), QR ** -0.5, 0.21875, ((0, 8), (1, 4)))
    latent_down = noise(keys[6], (D, KVR + ROPE), D ** -0.5, 0.125, ((0, 32),))
    latent_gain = jnp.clip(1.0 + 0.1 * jax.random.normal(keys[7], (KVR,), jnp.float32), 0.5, 1.5).astype(jnp.bfloat16)
    latent_up = noise(keys[8], (KVR, H * (NOPE + VD)), KVR ** -0.5, 0.375, ((0, 8), (1, 4)))
    out_proj = noise(keys[9], (H * VD, D), (max(H * VD // SEQ_LEN, 1)) ** -0.5, 4.0, ((0, 4), (1, 8)))
    post_gain = jnp.clip(1.0 + 0.1 * jax.random.normal(keys[10], (D,), jnp.float32), 0.5, 1.5).astype(jnp.bfloat16)
    gate_proj = noise(keys[11], (D, FF), D ** -0.5, 0.125, ((0, 8), (1, 4)))
    up_proj = noise(keys[12], (D, FF), D ** -0.5, 0.125, ((0, 8), (1, 4)))
    down_proj = noise(keys[13], (FF, D), (max(FF // 128, 1)) ** -0.5, 0.875, ((0, 4), (1, 8)))
    cotangent = noise(keys[14], (MB, N_DP * SEQ_LEN, D), 1.0, 6.0, ((1, 32),))
    return dict(tokens=tokens, prefix=prefix, input_gain=input_gain, query_down=query_down, query_gain=query_gain, query_up=query_up, latent_down=latent_down, latent_gain=latent_gain, latent_up=latent_up, out_proj=out_proj, post_gain=post_gain, gate_proj=gate_proj, up_proj=up_proj, down_proj=down_proj, cotangent=cotangent)


EPSILON = 1e-05
RESIDUAL = 1.4 / math.sqrt(62.0)
NEGATIVE = -1e+30
ROPE_BASE = 10000.0

@jax.custom_vjp
def low(v):
    return lax.optimization_barrier(v.astype(jnp.bfloat16)).astype(jnp.float32)

@jax.custom_vjp
def low_back(v):
    return v

def low_keep(v):
    return (low(v), None)

def low_pass(kept, grad):
    return (grad,)

def back_keep(v):
    return (v, None)

def back_low(kept, grad):
    return (low(grad),)
low.defvjp(low_keep, low_pass)
low_back.defvjp(back_keep, back_low)

def matmul_high(left_side, right_side):
    return jnp.dot(left_side, right_side, precision=lax.Precision.HIGHEST)

def norm_rows(values, gain_vec):
    return values * lax.rsqrt(lax.optimization_barrier(jnp.mean(values * values, axis=-1, keepdims=True)) + EPSILON) * gain_vec

def rotary(row_count, row_start, rope_width):
    half_width = rope_width // 2
    frequency = ROPE_BASE ** (-2.0 * jnp.arange(half_width).astype(jnp.float32) / rope_width)
    angles = (row_start + jnp.arange(row_count)).astype(jnp.float32)[:, None] * frequency[None, :]
    return (jnp.cos(angles), jnp.sin(angles))

def rotate(values, cosine, sine_table):
    half_width = values.shape[-1] // 2
    first_half = values[..., :half_width]
    second_half = values[..., half_width:]
    return jnp.concatenate([first_half * cosine - second_half * sine_table, second_half * cosine + first_half * sine_table], axis=-1)

def sequence_layer(sequence, weights, prefix_len):
    input_gain, query_down, query_gain, query_up, latent_down, latent_gain, latent_up, out_proj, post_gain, gate_proj, up_proj, down_proj = weights
    seq_length = sequence.shape[0]
    cosine, sine_table = rotary(seq_length, 0, ROPE)
    normed = low(norm_rows(sequence, input_gain))
    query_lat = low_back(matmul_high(normed, query_down))
    query_comp = low(norm_rows(query_lat, query_gain))
    latent_all = low_back(matmul_high(normed, latent_down))
    latent_norm = low(norm_rows(latent_all[:, :KVR], latent_gain))
    key_rope = low(rotate(latent_all[:, KVR:], cosine, sine_table))
    query_raw = low_back(matmul_high(query_comp, query_up)).reshape(seq_length, H, NOPE + ROPE)
    queries = low(jnp.concatenate([query_raw[..., :NOPE], rotate(query_raw[..., NOPE:], cosine[:, None], sine_table[:, None])], axis=-1))
    keyval = low(low_back(matmul_high(latent_norm, latent_up))).reshape(seq_length, H, NOPE + VD)
    key_nope = keyval[..., :NOPE]
    values = keyval[..., NOPE:]
    block_rows = 512 if seq_length % 512 == 0 else seq_length
    block_count = seq_length // block_rows
    score_scale = (NOPE + ROPE) ** (-0.5)
    columns = jnp.arange(seq_length).astype(jnp.int32)

    def attend(block_item):
        query_part, row_start = block_item
        positions = row_start + jnp.arange(block_rows).astype(jnp.int32)
        visible = (columns[None, :] <= positions[:, None]) | (columns[None, :] < prefix_len)
        raw_scores = jnp.einsum('qhd,khd->hqk', query_part[..., :NOPE], key_nope, precision=lax.Precision.HIGHEST)
        raw_scores = raw_scores + jnp.einsum('qhd,kd->hqk', query_part[..., NOPE:], key_rope, precision=lax.Precision.HIGHEST)
        scores = low_back(jnp.where(visible[None], raw_scores * score_scale, NEGATIVE))
        row_peak = lax.optimization_barrier(jnp.max(scores, axis=-1, keepdims=True))
        exp_scores = jnp.exp(scores - row_peak)
        attn_probs = low(exp_scores / lax.optimization_barrier(jnp.sum(exp_scores, axis=-1, keepdims=True)))
        return jnp.einsum('hqk,khd->qhd', attn_probs, values, precision=lax.Precision.HIGHEST)
    starts = jnp.arange(block_count).astype(jnp.int32) * block_rows
    attended = lax.map(jax.checkpoint(attend), (queries.reshape(block_count, block_rows, H, NOPE + ROPE), starts))
    attn_flat = low(low_back(attended.reshape(seq_length, H * VD)))
    attn_rows = low_back(matmul_high(attn_flat, out_proj))
    middle = sequence + RESIDUAL * attn_rows
    hidden_in = low(norm_rows(middle, post_gain))
    gate_val = low_back(matmul_high(hidden_in, gate_proj))
    up_val = low_back(matmul_high(hidden_in, up_proj))
    active = low(gate_val * jax.nn.sigmoid(gate_val) * up_val)
    mlp_rows = low_back(matmul_high(active, down_proj))
    return middle + RESIDUAL * mlp_rows

def reference(tokens, prefix, input_gain, query_down, query_gain, query_up, latent_down, latent_gain, latent_up, out_proj, post_gain, gate_proj, up_proj, down_proj, cotangent):
    weights = tuple((weight_arg.astype(jnp.float32) for weight_arg in (input_gain, query_down, query_gain, query_up, latent_down, latent_gain, latent_up, out_proj, post_gain, gate_proj, up_proj, down_proj)))
    seq_count = MB * N_DP
    sequences = tokens.astype(jnp.float32).reshape(seq_count, SEQ_LEN, D)
    prefix_flat = prefix.reshape(seq_count).astype(jnp.int32)
    layer = jax.checkpoint(sequence_layer)

    def forward(seq_input, weight_input):

        def step(carried, block_item):
            return (carried, layer(block_item[0], weight_input, block_item[1]))
        unused, outputs = lax.scan(step, jnp.zeros((), jnp.float32), (seq_input, prefix_flat))
        return outputs
    outputs, pullback = jax.vjp(forward, sequences, weights)
    grad_seq, grad_weights = pullback(cotangent.astype(jnp.float32).reshape(seq_count, SEQ_LEN, D))
    shape_out = (MB, N_DP * SEQ_LEN, D)
    return (outputs.reshape(shape_out).astype(jnp.bfloat16), grad_seq.reshape(shape_out), grad_weights[0], grad_weights[1], grad_weights[2], grad_weights[3], grad_weights[4], grad_weights[5], grad_weights[6], grad_weights[7], grad_weights[8], grad_weights[9], grad_weights[10], grad_weights[11])
```

```python
import math

import jax
import jax.numpy as jnp
from jax import lax
from jax.experimental import pallas as pl
from jax.experimental.pallas import tpu as pltpu
from jax.sharding import Mesh
from jax.sharding import PartitionSpec as P

NOPE = 64
ROPE = 32
VD = 64
KVR = 256
HEAD = NOPE + ROPE
PREFIX_MAX = 512
BLOCK = 256

DP = ("ring", "core")
EVERYWHERE = ("ring", "core", "tensor")

EPSILON = 1e-05
RESIDUAL = 1.4 / math.sqrt(62.0)
NEGATIVE = -1e30
ROPE_BASE = 10000.0
SCALE = HEAD ** (-0.5)

BF16 = jnp.bfloat16
F32 = jnp.float32


def dot(left_side, right_side, left_dim, right_dim):
    return lax.dot_general(
        left_side, right_side, (((left_dim,), (right_dim,)), ((), ())), preferred_element_type=F32
    )


def inverse_rms(values):
    return lax.rsqrt(jnp.mean(values * values, axis=-1, keepdims=True) + EPSILON)


def norm_back(values, gain_vec, grad_out):
    scale_inv = inverse_rms(values)
    normal = values * scale_inv
    grad_norm = grad_out * gain_vec
    grad_values = scale_inv * (
        grad_norm - normal * jnp.mean(grad_norm * normal, axis=-1, keepdims=True)
    )
    return (grad_values, jnp.sum(grad_out * normal, axis=0))


def rotary(row_count, row_start):
    half_width = ROPE // 2
    frequency = ROPE_BASE ** (-2.0 * jnp.arange(half_width).astype(F32) / ROPE)
    angles = (row_start + jnp.arange(row_count)).astype(F32)[:, None] * frequency[None, :]
    return (jnp.cos(angles), jnp.sin(angles))


def rotate(values, cosine, sine_table, axis=-1):
    first_half, second_half = jnp.split(values, 2, axis=axis)
    return jnp.concatenate(
        [
            first_half * cosine - second_half * sine_table,
            second_half * cosine + first_half * sine_table,
        ],
        axis=axis,
    )


def key_width(block_index, seq_length):
    return min(max((block_index + 1) * BLOCK, PREFIX_MAX), seq_length)


def block_scores(keys, query_block, block_index, width, prefix_len):
    scores = jnp.dot(keys[:width], query_block, preferred_element_type=F32)
    first = block_index * BLOCK
    tail = scores[first:]
    key_at = first + lax.broadcasted_iota(jnp.int32, tail.shape, 0)
    query_at = first + lax.broadcasted_iota(jnp.int32, tail.shape, 1)
    tail = jnp.where((key_at <= query_at) | (key_at < prefix_len), tail, NEGATIVE)
    if first:
        return jnp.concatenate([scores[:first], tail], axis=0)
    return tail


def attend_kernel(prefix_ref, query_ref, keyval_ref, rope_ref, out_ref, log_ref):
    seq_length = query_ref.shape[-1]
    prefix_len = prefix_ref[0]
    keyval = keyval_ref[0]
    keys = jnp.concatenate([keyval[:NOPE], rope_ref[...]], axis=0).T
    values_t = keyval[NOPE:]
    for block_index in range(seq_length // BLOCK):
        at = pl.ds(block_index * BLOCK, BLOCK)
        width = key_width(block_index, seq_length)
        scores = block_scores(keys, query_ref[0, :, at], block_index, width, prefix_len)
        peak = jnp.max(scores, axis=0, keepdims=True)
        exp_scores = jnp.exp((scores - peak) * SCALE)
        total = jnp.sum(exp_scores, axis=0, keepdims=True)
        block_out = jnp.dot(
            values_t[:, :width], exp_scores.astype(BF16), preferred_element_type=F32
        )
        out_ref[0, :, at] = (block_out / total).astype(BF16)
        log_ref[0, :, at] = peak * SCALE + jnp.log(total)


def attend(prefix_len, queries_t, keyval_t, rope_t):
    heads, _, seq_length = queries_t.shape
    head_block = lambda rows: pl.BlockSpec((1, rows, seq_length), lambda h: (h, 0, 0))
    return pl.pallas_call(
        attend_kernel,
        grid=(heads,),
        in_specs=[
            pl.BlockSpec(memory_space=pltpu.SMEM),
            head_block(HEAD),
            head_block(NOPE + VD),
            pl.BlockSpec((ROPE, seq_length), lambda h: (0, 0)),
        ],
        out_specs=[head_block(VD), head_block(1)],
        out_shape=[
            jax.ShapeDtypeStruct((heads, VD, seq_length), BF16),
            jax.ShapeDtypeStruct((heads, 1, seq_length), F32),
        ],
        compiler_params=pltpu.CompilerParams(vmem_limit_bytes=40 * 2**20),
        cost_estimate=pl.CostEstimate(
            flops=2 * heads * seq_length * seq_length * 384,
            bytes_accessed=heads * seq_length * 600,
            transcendentals=heads * seq_length * seq_length,
        ),
        name="attend",
    )(prefix_len, queries_t, keyval_t, rope_t)


def attend_back_kernel(
    prefix_ref,
    query_ref,
    keyval_ref,
    rope_ref,
    grad_ref,
    log_ref,
    cos_ref,
    sin_ref,
    dquery_ref,
    dkeyval_ref,
    drope_ref,
    dkey_acc,
    dvalue_acc,
):
    seq_length = query_ref.shape[-1]
    prefix_len = prefix_ref[0]
    keyval = keyval_ref[0]
    keys_t = jnp.concatenate([keyval[:NOPE], rope_ref[...]], axis=0)
    keys = keys_t.T
    values = keyval[NOPE:].T
    dkey_acc[...] = jnp.zeros_like(dkey_acc)
    dvalue_acc[...] = jnp.zeros_like(dvalue_acc)
    for block_index in range(seq_length // BLOCK):
        at = pl.ds(block_index * BLOCK, BLOCK)
        width = key_width(block_index, seq_length)
        query_block = query_ref[0, :, at]
        grad_block = grad_ref[0, :, at]
        scores = block_scores(keys, query_block, block_index, width, prefix_len)
        soft = jnp.exp(scores * SCALE - log_ref[0, :, at])
        grad_probs = jnp.dot(values[:width], grad_block, preferred_element_type=F32)
        delta = jnp.sum(soft * grad_probs, axis=0, keepdims=True)
        grad_scores = (soft * (grad_probs - delta)).astype(BF16)
        dquery = SCALE * jnp.dot(keys_t[:, :width], grad_scores, preferred_element_type=F32)
        dquery_ref[0, :NOPE, at] = dquery[:NOPE].astype(BF16)
        dquery_ref[0, NOPE:, at] = rotate(
            dquery[NOPE:], cos_ref[:, at], -sin_ref[:, at], axis=0
        ).astype(BF16)
        dkey_acc[:, :width] += dot(query_block, grad_scores, 1, 1)
        dvalue_acc[:, :width] += dot(grad_block, soft.astype(BF16), 1, 1)
    dkeyval_ref[0, :NOPE, :] = (SCALE * dkey_acc[:NOPE, :]).astype(BF16)
    dkeyval_ref[0, NOPE:, :] = dvalue_acc[...].astype(BF16)
    rope_part = SCALE * dkey_acc[NOPE:, :]

    @pl.when(pl.program_id(0) == 0)
    def _():
        drope_ref[...] = rope_part

    @pl.when(pl.program_id(0) > 0)
    def _():
        drope_ref[...] += rope_part


def attend_back(prefix_len, queries_t, keyval_t, rope_t, grad_t, logs, cos_t, sin_t):
    heads, _, seq_length = queries_t.shape
    head_block = lambda rows: pl.BlockSpec((1, rows, seq_length), lambda h: (h, 0, 0))
    whole = lambda rows: pl.BlockSpec((rows, seq_length), lambda h: (0, 0))
    return pl.pallas_call(
        attend_back_kernel,
        grid=(heads,),
        in_specs=[
            pl.BlockSpec(memory_space=pltpu.SMEM),
            head_block(HEAD),
            head_block(NOPE + VD),
            whole(ROPE),
            head_block(VD),
            head_block(1),
            whole(ROPE // 2),
            whole(ROPE // 2),
        ],
        out_specs=[head_block(HEAD), head_block(NOPE + VD), whole(ROPE)],
        out_shape=[
            jax.ShapeDtypeStruct((heads, HEAD, seq_length), BF16),
            jax.ShapeDtypeStruct((heads, NOPE + VD, seq_length), BF16),
            jax.ShapeDtypeStruct((ROPE, seq_length), F32),
        ],
        scratch_shapes=[
            pltpu.VMEM((HEAD, seq_length), F32),
            pltpu.VMEM((VD, seq_length), F32),
        ],
        compiler_params=pltpu.CompilerParams(vmem_limit_bytes=40 * 2**20),
        cost_estimate=pl.CostEstimate(
            flops=2 * heads * seq_length * seq_length * 960,
            bytes_accessed=heads * seq_length * 1100,
            transcendentals=heads * seq_length * seq_length,
        ),
        name="attend_back",
    )(prefix_len, queries_t, keyval_t, rope_t, grad_t, logs, cos_t, sin_t)


def weight_grad_kernel(*refs):
    out_ref = refs[-1]
    pairs = len(refs) // 2
    total = None
    for left_ref, right_ref in zip(refs[:pairs], refs[pairs:]):
        term = dot(left_ref[...], right_ref[...], 0, 0)
        total = term if total is None else total + term
    out_ref[...] = total.astype(BF16)


def weight_grad(lefts, rights):
    tokens, rows = lefts[0].shape
    columns = rights[0].shape[1]
    tile = 512 if rows % 512 == 0 else rows
    return pl.pallas_call(
        weight_grad_kernel,
        grid=(rows // tile,),
        in_specs=[pl.BlockSpec((tokens, tile), lambda i: (0, i))] * len(lefts)
        + [pl.BlockSpec((tokens, columns), lambda i: (0, 0))] * len(rights),
        out_specs=pl.BlockSpec((tile, columns), lambda i: (i, 0)),
        out_shape=jax.ShapeDtypeStruct((rows, columns), BF16),
        compiler_params=pltpu.CompilerParams(vmem_limit_bytes=56 * 2**20),
        cost_estimate=pl.CostEstimate(
            flops=2 * len(lefts) * tokens * rows * columns,
            bytes_accessed=2 * (len(lefts) * tokens * (rows + columns) + rows * columns),
            transcendentals=0,
        ),
        name="weight_grad",
    )(*lefts, *rights)


def swap(values, bit):
    return lax.ppermute(values, "tensor", [(index, index ^ bit) for index in range(4)])


def gather_blocks(values, hold=()):
    half = values.shape[0] // 2
    from_x = swap(values, 1)
    from_y = swap(values, 2)
    if hold:
        from_x, from_y = after((from_x, from_y), *hold)
    far_top = swap(from_y[:half], 1)
    far_low = swap(from_x[half:], 2)
    return (values, from_x, far_top, far_low, from_y)


def two_by_two():
    return lax.axis_size("tensor") == 4


def gather_ring(values, hold=()):
    if not two_by_two():
        return lax.all_gather(values, "tensor", axis=0, tiled=True)
    return jnp.concatenate(gather_blocks(values, hold), axis=0)


def scatter_ring(part):
    if not two_by_two():
        total = part("all", None).astype(BF16)
        return lax.psum_scatter(total, "tensor", scatter_dimension=0, tiled=True).astype(F32)
    rx = swap(part("xd", 0).astype(BF16), 1)
    ry = swap(part("dy", 1).astype(BF16), 2)
    rows = rx.shape[0] // 2
    to_y = (part("y", 0) + rx[rows:].astype(F32)).astype(BF16)
    to_x = (part("x", 1) + ry[:rows].astype(F32)).astype(BF16)
    ry2 = swap(to_y, 2)
    rx2 = swap(to_x, 1)
    left = part("o", 0) + rx[:rows].astype(F32) + ry2.astype(F32)
    right = part("o", 1) + ry[rows:].astype(F32) + rx2.astype(F32)
    return jnp.concatenate([left, right], axis=-1)


RING = {"o": (0, 1), "x": (1, 1), "xd": (1, 2), "dy": (2, 2), "y": (3, 1)}
FLIP = {"o": 0, "x": 1, "d": 3, "y": 2}


def ring_rows(values, names, rows):
    if names == "all":
        return values
    start, count = RING[names]
    return values[start * rows : (start + count) * rows]


def half_rows(weight, half):
    if half is None:
        return weight
    size = weight.shape[0] // 2
    return weight[half * size : (half + 1) * size]


def half_columns(values, half):
    if half is None:
        return values
    split = round(values.shape[1] / 256) * 128
    return values[:, split:] if half else values[:, :split]


def after(values, *others):
    return lax.optimization_barrier((values, *others))[0]


def widen(values, columns):
    return jnp.pad(values, ((0, 0), (0, columns - values.shape[1])))


def swap_cores(values):
    return lax.ppermute(values, "core", [(0, 1), (1, 0)])


def gather_everywhere(values):
    if not two_by_two():
        return lax.all_gather(values, EVERYWHERE, axis=0, tiled=True)
    rows, columns = values.shape
    own = lax.all_gather(values, DP, axis=0, tiled=True)
    size = own.shape[0] // 2
    core = lax.axis_index("core")
    tensor_at = lax.axis_index("tensor")
    mine = gather_ring(lax.dynamic_slice_in_dim(own, core * size, size, 0))
    other = swap_cores(mine)
    result = jnp.zeros((2, size // rows, 4, rows, columns), values.dtype)
    for side, pieces in ((core, mine), (1 - core, other)):
        for index, bit in enumerate((0, 1, 3, 2)):
            piece = pieces[index * size : (index + 1) * size]
            result = lax.dynamic_update_slice(
                result,
                piece.reshape(1, size // rows, 1, rows, columns),
                (side, 0, tensor_at ^ bit, 0, 0),
            )
    return result.reshape(-1, columns)


def scatter_everywhere(values, last_after):
    if not two_by_two():
        return lax.psum_scatter(values, EVERYWHERE, scatter_dimension=0, tiled=True)
    columns = values.shape[1]
    ring = lax.axis_size("ring")
    rows = values.shape[0] // (ring * 8)
    core = lax.axis_index("core")
    tensor_at = lax.axis_index("tensor")
    blocks = values.reshape(ring, 2, 4, rows, columns)
    pick = lambda index: lax.dynamic_slice_in_dim(blocks, index, 1, 1)[:, 0]
    chip = pick(core).astype(F32) + swap_cores(pick(1 - core)).astype(F32)
    chip = chip.astype(BF16)

    def part(names, half):
        pieces = [
            lax.dynamic_slice_in_dim(chip, tensor_at ^ FLIP[name], 1, 1).reshape(-1, columns)
            for name in names
        ]
        return half_columns(jnp.concatenate(pieces, axis=0), half).astype(F32)

    mine = after(scatter_ring(part).astype(BF16), *last_after)
    return lax.psum_scatter(mine, "ring", scatter_dimension=0, tiled=True)


def body(
    tokens,
    prefix,
    input_gain,
    query_down,
    query_gain,
    query_up,
    latent_down,
    latent_gain,
    latent_up,
    out_proj,
    post_gain,
    gate_proj,
    up_proj,
    down_proj,
    cotangent,
):
    micros = range(tokens.shape[0])
    rows = tokens.shape[1]
    width = tokens.shape[2]
    tensor_at = lax.axis_index("tensor")
    devices = lax.axis_size(EVERYWHERE)
    dp_size = lax.axis_size(DP)
    seq_length = rows * lax.axis_size("tensor")
    query_rank = query_down.shape[1]
    latent_rank = latent_down.shape[1]
    down_rank = query_rank + latent_rank
    packed_width = -(-(down_rank + 3) // 128) * 128
    own_rows = input_gain.shape[0]
    query_own = query_gain.shape[0]
    latent_own = latent_gain.shape[0]

    def gather_dp(values):
        return lax.all_gather(values, DP, axis=0, tiled=True)

    def scatter_dp(values):
        return lax.psum_scatter(values, DP, scatter_dimension=0, tiled=True)

    small = jnp.zeros((own_rows,), BF16)
    small = small.at[:query_own].set(query_gain)
    small = small.at[query_own : query_own + latent_own].set(latent_gain)
    packed = gather_everywhere(
        widen(
            jnp.concatenate(
                [query_down, latent_down, input_gain[:, None], post_gain[:, None], small[:, None]],
                axis=1,
            ),
            packed_width,
        )
    )
    query_rows, query_columns = query_up.shape
    latent_rows, latent_columns = latent_up.shape
    ups = gather_dp(jnp.concatenate([widen(query_up, latent_columns), latent_up], axis=0))
    ups = ups.reshape(dp_size, query_rows + latent_rows, latent_columns)
    up_query = ups[:, :query_rows, :query_columns].reshape(-1, query_columns)
    up_latent = ups[:, query_rows:].reshape(-1, latent_columns)
    out_t = gather_dp(out_proj.T)
    proj_gate = gather_dp(gate_proj)
    proj_up = gather_dp(up_proj)
    down_t = gather_dp(down_proj.T)

    gains = packed[:, down_rank : down_rank + 3].astype(F32)
    gain_in = gains[:, 0]
    gain_post = gains[:, 1]
    small_all = gains[:, 2].reshape(devices, own_rows)
    gain_query = small_all[:, :query_own].reshape(query_rank)
    gain_latent = small_all[:, query_own : query_own + latent_own].reshape(KVR)

    first_row = tensor_at * rows
    cos_local, sin_local = rotary(rows, first_row)
    cos_all, sin_all = rotary(seq_length, 0)
    cos_t, sin_t = cos_all.T, sin_all.T
    heads = up_query.shape[1] // HEAD

    def true_order(values):
        if not two_by_two():
            return lax.all_gather(values, "tensor", axis=0, tiled=True)
        own, from_x, far_top, far_low, from_y = gather_blocks(values)
        far = jnp.concatenate([far_top, far_low], axis=0)
        result = jnp.zeros((seq_length, values.shape[1]), values.dtype)
        for bit, piece in ((0, own), (1, from_x), (2, from_y), (3, far)):
            result = lax.dynamic_update_slice(result, piece, ((tensor_at ^ bit) * rows, 0))
        return result

    def true_block(values, name, axis):
        return lax.dynamic_slice_in_dim(values, (tensor_at ^ FLIP[name]) * rows, rows, axis)

    def true_rows(values, names, axis):
        if names == "all":
            return values
        pieces = [true_block(values, name, axis) for name in names]
        return pieces[0] if len(pieces) == 1 else jnp.concatenate(pieces, axis=axis)

    residual = tokens.reshape(-1, width).astype(F32)
    normed = (residual * inverse_rms(residual) * gain_in).astype(BF16)
    lat = dot(normed, packed, 1, 0)
    query_lat = lat[:, :query_rank]
    latent_comp = lat[:, query_rank : query_rank + KVR]
    query_comp = (query_lat * inverse_rms(query_lat) * gain_query).astype(BF16)
    latent_norm = (latent_comp * inverse_rms(latent_comp) * gain_latent).astype(BF16)
    cos_both = jnp.concatenate([cos_local for micro in micros], axis=0)
    sin_both = jnp.concatenate([sin_local for micro in micros], axis=0)
    key_rope = rotate(lat[:, query_rank + KVR : down_rank], cos_both, sin_both).astype(BF16)
    latents = jnp.concatenate([query_comp, latent_norm, key_rope], axis=1)

    def of_micro(values, micro):
        return values[micro * rows : (micro + 1) * rows]

    state = []
    for micro in micros:
        full = true_order(of_micro(latents, micro))
        state.append(
            dict(
                query_full=full[:, :query_rank],
                latent_full=full[:, query_rank : query_rank + KVR],
                rope_t=full[:, query_rank + KVR :].T,
            )
        )

    def gather_branch(micro, start_after, hold):
        branch = (RESIDUAL * cotangent[micro].astype(F32)).astype(BF16)
        return gather_ring(after(branch, start_after), (hold,))

    for micro in micros:
        st = state[micro]
        raw_t = dot(up_query, st["query_full"], 0, 1).reshape(heads, HEAD, seq_length)
        st["queries_t"] = jnp.concatenate(
            [raw_t[:, :NOPE], rotate(raw_t[:, NOPE:], cos_t[None], sin_t[None], axis=1)], axis=1
        ).astype(BF16)
        st["keyval_t"] = (
            dot(up_latent, st["latent_full"], 0, 1)
            .astype(BF16)
            .reshape(heads, NOPE + VD, seq_length)
        )
        attended_t, st["logs"] = attend(
            prefix[micro], st["queries_t"], st["keyval_t"], st["rope_t"]
        )
        st["attended_t"] = attended_t.reshape(heads * VD, seq_length)
        attn_rows = scatter_ring(
            lambda names, half: dot(
                true_rows(st["attended_t"], names, 1), half_rows(out_t, half), 0, 1
            )
        )
        st["middle"] = tokens[micro].astype(F32) + RESIDUAL * attn_rows
        hidden_in = (st["middle"] * inverse_rms(st["middle"]) * gain_post).astype(BF16)
        st["hidden"] = gather_ring(hidden_in)

    state[0]["branch"] = gather_branch(0, state[1]["query_full"], state[0]["attended_t"])

    def add_micros(term):
        total = term(state[0])
        for micro in micros[1:]:
            total = total + term(state[micro])
        return total.astype(BF16)

    state[0]["hidden"] = after(state[0]["hidden"], *[st["attended_t"] for st in state[1:]])
    for micro in micros:
        st = state[micro]
        gate_val = dot(st["hidden"], proj_gate, 1, 0).astype(BF16)
        up_val = dot(st["hidden"], proj_up, 1, 0).astype(BF16)
        gate_val, up_val = lax.optimization_barrier((gate_val, up_val))
        st["gate"], st["up"] = gate_val, up_val
        st["active"] = after(
            (jax.nn.silu(gate_val.astype(F32)) * up_val.astype(F32)).astype(BF16)
        )
    for micro in micros[1:]:
        state[micro]["branch"] = gather_branch(micro, state[0]["hidden"], state[0]["active"])

    def both(name):
        return [st[name] for st in state]

    down_part = weight_grad(both("branch"), both("active"))
    down_grad = scatter_dp(down_part)

    for micro in micros:
        st = state[micro]
        gate_val, up_val = st["gate"].astype(F32), st["up"].astype(F32)
        sigmoid_gate = jax.nn.sigmoid(gate_val)
        grad_active = dot(st["branch"], down_t, 1, 0)
        grad_gate = (
            grad_active * up_val * sigmoid_gate * (1.0 + gate_val * (1.0 - sigmoid_gate))
        ).astype(BF16)
        grad_up = (grad_active * gate_val * sigmoid_gate).astype(BF16)
        grad_gate, grad_up = after((grad_gate, grad_up), down_part)
        st["grad_gate"], st["grad_up"] = grad_gate, grad_up
        grad_hidden = scatter_ring(
            lambda names, half: dot(
                ring_rows(grad_gate, names, rows), half_rows(proj_gate, half), 1, 1
            )
            + dot(ring_rows(grad_up, names, rows), half_rows(proj_up, half), 1, 1)
        )
        grad_mid_norm, st["post_gain_grad"] = norm_back(st["middle"], gain_post, grad_hidden)
        st["grad_mid"] = cotangent[micro].astype(F32) + grad_mid_norm
        st["attn_grad"] = true_order((RESIDUAL * st["grad_mid"]).astype(BF16))
    gate_part = weight_grad(both("hidden"), both("grad_gate"))
    gate_grad = scatter_dp(after(gate_part, down_grad))
    up_part = weight_grad(both("hidden"), both("grad_up"))
    up_grad = scatter_dp(after(up_part, gate_grad))

    for micro in micros:
        st = state[micro]
        attn_grad = after(st["attn_grad"], gate_part, up_part)
        grad_t = dot(out_t, attn_grad, 0, 1).astype(BF16).reshape(heads, VD, seq_length)
        dquery_t, dkeyval_t, drope_t = attend_back(
            prefix[micro],
            st["queries_t"],
            st["keyval_t"],
            st["rope_t"],
            grad_t,
            st["logs"],
            cos_t,
            sin_t,
        )
        st["dquery_t"] = dquery_t.reshape(heads * HEAD, seq_length)
        st["dkeyval_t"] = dkeyval_t.reshape(heads * (NOPE + VD), seq_length)
        comp_part = dot(st["dquery_t"], up_query, 0, 1)
        norm_part = dot(st["dkeyval_t"], up_latent, 0, 1)
        latent_part = jnp.concatenate(
            [comp_part.astype(BF16), norm_part.astype(BF16), drope_t.T.astype(BF16)], axis=1
        )
        st["grad_lat"] = scatter_ring(
            lambda names, half: true_rows(half_columns(latent_part, half), names, 0).astype(F32)
        )

    out_part = add_micros(lambda st: dot(st["attn_grad"], st["attended_t"], 0, 1))
    out_grad = scatter_dp(after(out_part, up_grad))
    query_up_part = add_micros(lambda st: dot(st["query_full"], st["dquery_t"], 0, 1))
    latent_up_part = add_micros(lambda st: dot(st["latent_full"], st["dkeyval_t"], 0, 1))
    ups_part = jnp.concatenate(
        [
            widen(query_up_part, latent_columns).reshape(dp_size, query_rows, latent_columns),
            latent_up_part.reshape(dp_size, latent_rows, latent_columns),
        ],
        axis=1,
    ).reshape(-1, latent_columns)
    ups_grad = scatter_dp(after(ups_part, out_grad))

    grad_lat = jnp.concatenate([st["grad_lat"] for st in state], axis=0)
    grad_qlat, query_gain_grad = norm_back(query_lat, gain_query, grad_lat[:, :query_rank])
    grad_comp, latent_gain_grad = norm_back(
        latent_comp, gain_latent, grad_lat[:, query_rank : query_rank + KVR]
    )
    grad_rope = rotate(grad_lat[:, query_rank + KVR :], cos_both, -sin_both)
    grad_down = widen(
        jnp.concatenate(
            [grad_qlat.astype(BF16), grad_comp.astype(BF16), grad_rope.astype(BF16)], axis=1
        ),
        packed_width,
    )
    grad_normed = dot(grad_down, packed, 1, 1)
    grad_resid, input_gain_grad = norm_back(residual, gain_in, grad_normed)
    small_grad = jnp.concatenate(
        [
            query_gain_grad.reshape(devices, query_own),
            latent_gain_grad.reshape(devices, latent_own),
            jnp.zeros((devices, own_rows - query_own - latent_own), F32),
        ],
        axis=1,
    ).reshape(width)
    post_gain_grad = sum(st["post_gain_grad"] for st in state)
    vectors = jnp.stack([input_gain_grad, post_gain_grad, small_grad], axis=1)
    vectors = jnp.pad(vectors, ((0, 0), (down_rank, packed_width - down_rank - 3)))
    packed_grad = scatter_everywhere(
        (dot(normed, grad_down, 0, 0) + vectors).astype(BF16), (ups_grad,)
    )
    packed_grad = packed_grad.astype(F32)
    d_tokens = [
        st["grad_mid"] + of_micro(grad_resid, micro) for micro, st in enumerate(state)
    ]

    mixed = []
    for micro in micros:
        st = state[micro]
        active = after(st["active"], state[-1]["attn_grad"])
        mlp_rows = scatter_ring(
            lambda names, half: dot(
                ring_rows(active, names, rows), half_rows(down_t, half), 1, 1
            )
        )
        mixed.append((st["middle"] + RESIDUAL * mlp_rows).astype(BF16))

    small_grad = packed_grad[:, down_rank + 2]
    return (
        jnp.stack(mixed, axis=0),
        jnp.stack(d_tokens, axis=0),
        packed_grad[:, down_rank],
        packed_grad[:, :query_rank],
        small_grad[:query_own],
        ups_grad[:query_rows, :query_columns].astype(F32),
        packed_grad[:, query_rank:down_rank],
        small_grad[query_own : query_own + latent_own],
        ups_grad[query_rows:].astype(F32),
        out_grad.T.astype(F32),
        packed_grad[:, down_rank + 1],
        gate_grad.astype(F32),
        up_grad.astype(F32),
        down_grad.T.astype(F32),
    )


def solution(mesh):
    dp_size, tensor_size = mesh.devices.shape
    mesh = Mesh(mesh.devices.reshape(dp_size // 2, 2, tensor_size), EVERYWHERE)
    return jax.shard_map(
        body,
        mesh=mesh,
        in_specs=(
            P(None, EVERYWHERE, None),
            P(None, DP),
            P(EVERYWHERE),
            P(EVERYWHERE, None),
            P(EVERYWHERE),
            P(DP, "tensor"),
            P(EVERYWHERE, None),
            P(EVERYWHERE),
            P(DP, "tensor"),
            P("tensor", DP),
            P(EVERYWHERE),
            P(DP, "tensor"),
            P(DP, "tensor"),
            P("tensor", DP),
            P(None, EVERYWHERE, None),
        ),
        out_specs=(
            P(None, EVERYWHERE, None),
            P(None, EVERYWHERE, None),
            P(EVERYWHERE),
            P(EVERYWHERE, None),
            P(EVERYWHERE),
            P(DP, "tensor"),
            P(EVERYWHERE, None),
            P(EVERYWHERE),
            P(DP, "tensor"),
            P("tensor", DP),
            P(EVERYWHERE),
            P(DP, "tensor"),
            P(DP, "tensor"),
            P("tensor", DP),
        ),
        check_vma=False,
    )
```

```python
import functools
import math

import jax
import jax.numpy as jnp
from jax import lax
from jax.experimental import pallas as pl
from jax.experimental.pallas import tpu as pltpu
from jax.sharding import Mesh
from jax.sharding import PartitionSpec as P

NOPE = 64
ROPE = 32
VD = 64
KVR = 256
HEAD = NOPE + ROPE
PREFIX_MAX = 512
BLOCK = 256

DP = ("ring", "core")
EVERYWHERE = ("ring", "core", "tensor")

EPSILON = 1e-05
RESIDUAL = 1.4 / math.sqrt(62.0)
NEGATIVE = -1e30
ROPE_BASE = 10000.0
SCALE = HEAD ** (-0.5)

BF16 = jnp.bfloat16
F32 = jnp.float32


def dot(left_side, right_side, left_dim, right_dim):
    return lax.dot_general(
        left_side, right_side, (((left_dim,), (right_dim,)), ((), ())), preferred_element_type=F32
    )


def inverse_rms(values):
    return lax.rsqrt(jnp.mean(values * values, axis=-1, keepdims=True) + EPSILON)


def norm_back(values, gain_vec, grad_out):
    scale_inv = inverse_rms(values)
    normal = values * scale_inv
    grad_norm = grad_out * gain_vec
    grad_values = scale_inv * (
        grad_norm - normal * jnp.mean(grad_norm * normal, axis=-1, keepdims=True)
    )
    return (grad_values, jnp.sum(grad_out * normal, axis=0))


def rotary(row_count, row_start):
    half_width = ROPE // 2
    frequency = ROPE_BASE ** (-2.0 * jnp.arange(half_width).astype(F32) / ROPE)
    angles = (row_start + jnp.arange(row_count)).astype(F32)[:, None] * frequency[None, :]
    return (jnp.cos(angles), jnp.sin(angles))


def rotate(values, cosine, sine_table, axis=-1):
    first_half, second_half = jnp.split(values, 2, axis=axis)
    return jnp.concatenate(
        [
            first_half * cosine - second_half * sine_table,
            second_half * cosine + first_half * sine_table,
        ],
        axis=axis,
    )


def key_width(block_index, seq_length):
    return min(max((block_index + 1) * BLOCK, PREFIX_MAX), seq_length)


def block_scores(keys, query_block, block_index, width, prefix_len):
    scores = jnp.dot(keys[:width], query_block, preferred_element_type=F32)
    first = block_index * BLOCK
    tail = scores[first:]
    key_at = first + lax.broadcasted_iota(jnp.int32, tail.shape, 0)
    query_at = first + lax.broadcasted_iota(jnp.int32, tail.shape, 1)
    tail = jnp.where((key_at <= query_at) | (key_at < prefix_len), tail, NEGATIVE)
    if first:
        return jnp.concatenate([scores[:first], tail], axis=0)
    return tail


def attend_kernel(prefix_ref, query_ref, keyval_ref, rope_ref, out_ref, log_ref):
    seq_length = query_ref.shape[-1]
    prefix_len = prefix_ref[0]
    keyval = keyval_ref[0]
    keys = jnp.concatenate([keyval[:NOPE], rope_ref[...]], axis=0).T
    values_t = keyval[NOPE:]
    for block_index in range(seq_length // BLOCK):
        at = pl.ds(block_index * BLOCK, BLOCK)
        width = key_width(block_index, seq_length)
        scores = block_scores(keys, query_ref[0, :, at], block_index, width, prefix_len)
        peak = jnp.max(scores, axis=0, keepdims=True)
        exp_scores = jnp.exp((scores - peak) * SCALE)
        total = jnp.sum(exp_scores, axis=0, keepdims=True)
        block_out = jnp.dot(
            values_t[:, :width], exp_scores.astype(BF16), preferred_element_type=F32
        )
        out_ref[0, :, at] = (block_out / total).astype(BF16)
        log_ref[0, :, at] = peak * SCALE + jnp.log(total)


def attend(prefix_len, queries_t, keyval_t, rope_t):
    heads, _, seq_length = queries_t.shape
    head_block = lambda rows: pl.BlockSpec((1, rows, seq_length), lambda h: (h, 0, 0))
    return pl.pallas_call(
        attend_kernel,
        grid=(heads,),
        in_specs=[
            pl.BlockSpec(memory_space=pltpu.SMEM),
            head_block(HEAD),
            head_block(NOPE + VD),
            pl.BlockSpec((ROPE, seq_length), lambda h: (0, 0)),
        ],
        out_specs=[head_block(VD), head_block(1)],
        out_shape=[
            jax.ShapeDtypeStruct((heads, VD, seq_length), BF16),
            jax.ShapeDtypeStruct((heads, 1, seq_length), F32),
        ],
        compiler_params=pltpu.CompilerParams(vmem_limit_bytes=40 * 2**20),
        cost_estimate=pl.CostEstimate(
            flops=2 * heads * seq_length * seq_length * 384,
            bytes_accessed=heads * seq_length * 600,
            transcendentals=heads * seq_length * seq_length,
        ),
        name="attend",
    )(prefix_len, queries_t, keyval_t, rope_t)


def attend_back_kernel(
    prefix_ref,
    query_ref,
    keyval_ref,
    rope_ref,
    grad_ref,
    log_ref,
    cos_ref,
    sin_ref,
    *refs,
):
    dquery_ref, dkeyval_ref, drope_ref, dkey_acc, dvalue_acc = refs[-5:]
    seq_length = query_ref.shape[-1]
    prefix_len = prefix_ref[0]
    keyval = keyval_ref[0]
    keys_t = jnp.concatenate([keyval[:NOPE], rope_ref[...]], axis=0)
    keys = keys_t.T
    values = keyval[NOPE:].T
    dkey_acc[...] = jnp.zeros_like(dkey_acc)
    dvalue_acc[...] = jnp.zeros_like(dvalue_acc)
    for block_index in range(seq_length // BLOCK):
        at = pl.ds(block_index * BLOCK, BLOCK)
        width = key_width(block_index, seq_length)
        query_block = query_ref[0, :, at]
        grad_block = grad_ref[0, :, at]
        scores = block_scores(keys, query_block, block_index, width, prefix_len)
        soft = jnp.exp(scores * SCALE - log_ref[0, :, at])
        grad_probs = jnp.dot(values[:width], grad_block, preferred_element_type=F32)
        delta = jnp.sum(soft * grad_probs, axis=0, keepdims=True)
        grad_scores = (soft * (grad_probs - delta)).astype(BF16)
        dquery = SCALE * jnp.dot(keys_t[:, :width], grad_scores, preferred_element_type=F32)
        dquery_ref[0, :NOPE, at] = dquery[:NOPE].astype(BF16)
        dquery_ref[0, NOPE:, at] = rotate(
            dquery[NOPE:], cos_ref[:, at], -sin_ref[:, at], axis=0
        ).astype(BF16)
        dkey_acc[:, :width] += dot(query_block, grad_scores, 1, 1)
        dvalue_acc[:, :width] += dot(grad_block, soft.astype(BF16), 1, 1)
    dkeyval_ref[0, :NOPE, :] = (SCALE * dkey_acc[:NOPE, :]).astype(BF16)
    dkeyval_ref[0, NOPE:, :] = dvalue_acc[...].astype(BF16)
    rope_part = SCALE * dkey_acc[NOPE:, :]

    @pl.when(pl.program_id(0) == 0)
    def _():
        drope_ref[...] = rope_part

    @pl.when(pl.program_id(0) > 0)
    def _():
        drope_ref[...] += rope_part


def attend_back(prefix_len, queries_t, keyval_t, rope_t, grad_t, logs, cos_t, sin_t, *others):
    heads, _, seq_length = queries_t.shape
    head_block = lambda rows: pl.BlockSpec((1, rows, seq_length), lambda h: (h, 0, 0))
    whole = lambda rows: pl.BlockSpec((rows, seq_length), lambda h: (0, 0))
    return pl.pallas_call(
        attend_back_kernel,
        grid=(heads,),
        in_specs=[
            pl.BlockSpec(memory_space=pltpu.SMEM),
            head_block(HEAD),
            head_block(NOPE + VD),
            whole(ROPE),
            head_block(VD),
            head_block(1),
            whole(ROPE // 2),
            whole(ROPE // 2),
            *[pl.BlockSpec(memory_space=pl.ANY) for other in others],
        ],
        out_specs=[head_block(HEAD), head_block(NOPE + VD), whole(ROPE)],
        out_shape=[
            jax.ShapeDtypeStruct((heads, HEAD, seq_length), BF16),
            jax.ShapeDtypeStruct((heads, NOPE + VD, seq_length), BF16),
            jax.ShapeDtypeStruct((ROPE, seq_length), F32),
        ],
        scratch_shapes=[
            pltpu.VMEM((HEAD, seq_length), F32),
            pltpu.VMEM((VD, seq_length), F32),
        ],
        compiler_params=pltpu.CompilerParams(vmem_limit_bytes=40 * 2**20),
        cost_estimate=pl.CostEstimate(
            flops=2 * heads * seq_length * seq_length * 960,
            bytes_accessed=heads * seq_length * 1100,
            transcendentals=heads * seq_length * seq_length,
        ),
        name="attend_back",
    )(prefix_len, queries_t, keyval_t, rope_t, grad_t, logs, cos_t, sin_t, *others)


def weight_grad_kernel(*refs):
    out_ref = refs[-1]
    pairs = len(refs) // 2
    total = None
    for left_ref, right_ref in zip(refs[:pairs], refs[pairs:]):
        term = dot(left_ref[...], right_ref[...], 0, 0)
        total = term if total is None else total + term
    out_ref[...] = total.astype(BF16)


def weight_grad(lefts, rights):
    tokens, rows = lefts[0].shape
    columns = rights[0].shape[1]
    tile = 512 if rows % 512 == 0 else rows
    return pl.pallas_call(
        weight_grad_kernel,
        grid=(rows // tile,),
        in_specs=[pl.BlockSpec((tokens, tile), lambda i: (0, i))] * len(lefts)
        + [pl.BlockSpec((tokens, columns), lambda i: (0, 0))] * len(rights),
        out_specs=pl.BlockSpec((tile, columns), lambda i: (i, 0)),
        out_shape=jax.ShapeDtypeStruct((rows, columns), BF16),
        compiler_params=pltpu.CompilerParams(vmem_limit_bytes=56 * 2**20),
        cost_estimate=pl.CostEstimate(
            flops=2 * len(lefts) * tokens * rows * columns,
            bytes_accessed=2 * (len(lefts) * tokens * (rows + columns) + rows * columns),
            transcendentals=0,
        ),
        name="weight_grad",
    )(*lefts, *rights)


def swap(values, bit):
    return lax.ppermute(values, "tensor", [(index, index ^ bit) for index in range(4)])


def gather_blocks(values, hold=()):
    half = values.shape[0] // 2
    from_x = swap(values, 1)
    from_y = swap(values, 2)
    if hold:
        from_x, from_y = after((from_x, from_y), *hold)
    far_top = swap(from_y[:half], 1)
    far_low = swap(from_x[half:], 2)
    return (values, from_x, far_top, far_low, from_y)


def two_by_two():
    return lax.axis_size("tensor") == 4


def gather_ring(values, hold=()):
    if not two_by_two():
        return lax.all_gather(values, "tensor", axis=0, tiled=True)
    return jnp.concatenate(gather_blocks(values, hold), axis=0)


def scatter_ring(part):
    if not two_by_two():
        total = part("all", None).astype(BF16)
        return lax.psum_scatter(total, "tensor", scatter_dimension=0, tiled=True).astype(F32)
    rx = swap(part("xd", 0).astype(BF16), 1)
    ry = swap(part("dy", 1).astype(BF16), 2)
    rows = rx.shape[0] // 2
    to_y = (part("y", 0) + rx[rows:].astype(F32)).astype(BF16)
    to_x = (part("x", 1) + ry[:rows].astype(F32)).astype(BF16)
    ry2 = swap(to_y, 2)
    rx2 = swap(to_x, 1)
    left = part("o", 0) + rx[:rows].astype(F32) + ry2.astype(F32)
    right = part("o", 1) + ry[rows:].astype(F32) + rx2.astype(F32)
    return jnp.concatenate([left, right], axis=-1)


RING = {"o": (0, 1), "x": (1, 1), "xd": (1, 2), "dy": (2, 2), "y": (3, 1)}
FLIP = {"o": 0, "x": 1, "d": 3, "y": 2}


def ring_rows(values, names, rows):
    if names == "all":
        return values
    start, count = RING[names]
    return values[start * rows : (start + count) * rows]


def half_rows(weight, half):
    if half is None:
        return weight
    size = weight.shape[0] // 2
    return weight[half * size : (half + 1) * size]


def half_columns(values, half):
    if half is None:
        return values
    split = round(values.shape[1] / 256) * 128
    return values[:, split:] if half else values[:, :split]


def after(values, *others):
    return lax.optimization_barrier((values, *others))[0]


def nothing_kernel(*refs):
    pass


def tie(values, *others):
    if not others:
        return values
    anywhere = pl.BlockSpec(memory_space=pl.ANY)
    return pl.pallas_call(
        nothing_kernel,
        in_specs=[anywhere] * (1 + len(others)),
        out_specs=anywhere,
        out_shape=jax.ShapeDtypeStruct(values.shape, values.dtype),
        input_output_aliases={0: 0},
        name="tie",
    )(values, *others)


def widen(values, columns):
    return jnp.pad(values, ((0, 0), (0, columns - values.shape[1])))


def swap_cores(values):
    return lax.ppermute(values, "core", [(0, 1), (1, 0)])


def gather_everywhere(values):
    if not two_by_two():
        return lax.all_gather(values, EVERYWHERE, axis=0, tiled=True)
    rows, columns = values.shape
    own = lax.all_gather(values, DP, axis=0, tiled=True)
    size = own.shape[0] // 2
    core = lax.axis_index("core")
    tensor_at = lax.axis_index("tensor")
    mine = gather_ring(lax.dynamic_slice_in_dim(own, core * size, size, 0))
    other = swap_cores(mine)
    result = jnp.zeros((2, size // rows, 4, rows, columns), values.dtype)
    for side, pieces in ((core, mine), (1 - core, other)):
        for index, bit in enumerate((0, 1, 3, 2)):
            piece = pieces[index * size : (index + 1) * size]
            result = lax.dynamic_update_slice(
                result,
                piece.reshape(1, size // rows, 1, rows, columns),
                (side, 0, tensor_at ^ bit, 0, 0),
            )
    return result.reshape(-1, columns)


def scatter_everywhere(values, last_after):
    if not two_by_two():
        return lax.psum_scatter(values, EVERYWHERE, scatter_dimension=0, tiled=True)
    columns = values.shape[1]
    ring = lax.axis_size("ring")
    rows = values.shape[0] // (ring * 8)
    core = lax.axis_index("core")
    tensor_at = lax.axis_index("tensor")
    blocks = values.reshape(ring, 2, 4, rows, columns)
    pick = lambda index: lax.dynamic_slice_in_dim(blocks, index, 1, 1)[:, 0]
    chip = pick(core).astype(F32) + swap_cores(pick(1 - core)).astype(F32)
    chip = chip.astype(BF16)

    def part(names, half):
        pieces = [
            lax.dynamic_slice_in_dim(chip, tensor_at ^ FLIP[name], 1, 1).reshape(-1, columns)
            for name in names
        ]
        return half_columns(jnp.concatenate(pieces, axis=0), half).astype(F32)

    mine = after(scatter_ring(part).astype(BF16), *last_after)
    return lax.psum_scatter(mine, "ring", scatter_dimension=0, tiled=True)


def body(
    tokens,
    prefix,
    input_gain,
    query_down,
    query_gain,
    query_up,
    latent_down,
    latent_gain,
    latent_up,
    out_proj,
    post_gain,
    gate_proj,
    up_proj,
    down_proj,
    cotangent,
):
    micros = range(tokens.shape[0])
    rows = tokens.shape[1]
    width = tokens.shape[2]
    tensor_at = lax.axis_index("tensor")
    devices = lax.axis_size(EVERYWHERE)
    dp_size = lax.axis_size(DP)
    seq_length = rows * lax.axis_size("tensor")
    query_rank = query_down.shape[1]
    latent_rank = latent_down.shape[1]
    down_rank = query_rank + latent_rank
    packed_width = -(-(down_rank + 3) // 128) * 128
    own_rows = input_gain.shape[0]
    query_own = query_gain.shape[0]
    latent_own = latent_gain.shape[0]

    def gather_dp(values):
        return lax.all_gather(values, DP, axis=0, tiled=True)

    def scatter_dp(values):
        return lax.psum_scatter(values, DP, scatter_dimension=0, tiled=True)

    small = jnp.zeros((own_rows,), BF16)
    small = small.at[:query_own].set(query_gain)
    small = small.at[query_own : query_own + latent_own].set(latent_gain)
    packed = gather_everywhere(
        widen(
            jnp.concatenate(
                [query_down, latent_down, input_gain[:, None], post_gain[:, None], small[:, None]],
                axis=1,
            ),
            packed_width,
        )
    )
    query_rows, query_columns = query_up.shape
    latent_rows, latent_columns = latent_up.shape
    ups = gather_dp(jnp.concatenate([widen(query_up, latent_columns), latent_up], axis=0))
    ups = ups.reshape(dp_size, query_rows + latent_rows, latent_columns)
    up_query = ups[:, :query_rows, :query_columns].reshape(-1, query_columns)
    up_latent = ups[:, query_rows:].reshape(-1, latent_columns)
    out_t = gather_dp(out_proj.T)
    proj_gate = gather_dp(gate_proj)
    proj_up = gather_dp(up_proj)
    down_t = gather_dp(down_proj.T)

    gains = packed[:, down_rank : down_rank + 3].astype(F32)
    gain_in = gains[:, 0]
    gain_post = gains[:, 1]
    small_all = gains[:, 2].reshape(devices, own_rows)
    gain_query = small_all[:, :query_own].reshape(query_rank)
    gain_latent = small_all[:, query_own : query_own + latent_own].reshape(KVR)

    first_row = tensor_at * rows
    cos_local, sin_local = rotary(rows, first_row)
    cos_all, sin_all = rotary(seq_length, 0)
    cos_t, sin_t = cos_all.T, sin_all.T
    heads = up_query.shape[1] // HEAD

    def true_order(values):
        if not two_by_two():
            return lax.all_gather(values, "tensor", axis=0, tiled=True)
        own, from_x, far_top, far_low, from_y = gather_blocks(values)
        far = jnp.concatenate([far_top, far_low], axis=0)
        result = jnp.zeros((seq_length, values.shape[1]), values.dtype)
        for bit, piece in ((0, own), (1, from_x), (2, from_y), (3, far)):
            result = lax.dynamic_update_slice(result, piece, ((tensor_at ^ bit) * rows, 0))
        return result

    def true_block(values, name, axis):
        return lax.dynamic_slice_in_dim(values, (tensor_at ^ FLIP[name]) * rows, rows, axis)

    def true_rows(values, names, axis):
        if names == "all":
            return values
        pieces = [true_block(values, name, axis) for name in names]
        return pieces[0] if len(pieces) == 1 else jnp.concatenate(pieces, axis=axis)

    residual = tokens.reshape(-1, width).astype(F32)
    normed = (residual * inverse_rms(residual) * gain_in).astype(BF16)
    lat = dot(normed, packed, 1, 0)
    query_lat = lat[:, :query_rank]
    latent_comp = lat[:, query_rank : query_rank + KVR]
    query_comp = (query_lat * inverse_rms(query_lat) * gain_query).astype(BF16)
    latent_norm = (latent_comp * inverse_rms(latent_comp) * gain_latent).astype(BF16)
    cos_both = jnp.concatenate([cos_local for micro in micros], axis=0)
    sin_both = jnp.concatenate([sin_local for micro in micros], axis=0)
    key_rope = rotate(lat[:, query_rank + KVR : down_rank], cos_both, sin_both).astype(BF16)
    latents = jnp.concatenate([query_comp, latent_norm, key_rope], axis=1)

    def of_micro(values, micro):
        return values[micro * rows : (micro + 1) * rows]

    state = []
    for micro in micros:
        full = true_order(of_micro(latents, micro))
        state.append(
            dict(
                query_full=full[:, :query_rank],
                latent_full=full[:, query_rank : query_rank + KVR],
                rope_t=full[:, query_rank + KVR :].T,
            )
        )

    def gather_branch(micro, start_after, hold):
        branch = (RESIDUAL * cotangent[micro].astype(F32)).astype(BF16)
        return gather_ring(tie(branch, start_after), (hold,))

    for micro in micros:
        st = state[micro]
        raw_t = dot(up_query, st["query_full"], 0, 1).reshape(heads, HEAD, seq_length)
        st["queries_t"] = jnp.concatenate(
            [raw_t[:, :NOPE], rotate(raw_t[:, NOPE:], cos_t[None], sin_t[None], axis=1)], axis=1
        ).astype(BF16)
        st["keyval_t"] = (
            dot(up_latent, st["latent_full"], 0, 1)
            .astype(BF16)
            .reshape(heads, NOPE + VD, seq_length)
        )
        attended_t, st["logs"] = attend(
            prefix[micro], st["queries_t"], st["keyval_t"], st["rope_t"]
        )
        st["attended_t"] = attended_t.reshape(heads * VD, seq_length)
        attn_rows = scatter_ring(
            lambda names, half: dot(
                true_rows(st["attended_t"], names, 1), half_rows(out_t, half), 0, 1
            )
        )
        st["middle"] = tokens[micro].astype(F32) + RESIDUAL * attn_rows
        hidden_in = (st["middle"] * inverse_rms(st["middle"]) * gain_post).astype(BF16)
        st["hidden"] = gather_ring(hidden_in)

    state[0]["branch"] = gather_branch(0, state[1]["query_full"], state[0]["attended_t"])

    def add_micros(term):
        total = term(state[0])
        for micro in micros[1:]:
            total = total + term(state[micro])
        return total.astype(BF16)

    state[0]["hidden"] = after(state[0]["hidden"], *[st["attended_t"] for st in state[1:]])
    for micro in micros:
        st = state[micro]
        gate_val = dot(st["hidden"], proj_gate, 1, 0).astype(BF16)
        up_val = dot(st["hidden"], proj_up, 1, 0).astype(BF16)
        gate_val, up_val = lax.optimization_barrier((gate_val, up_val))
        st["gate"], st["up"] = gate_val, up_val
        st["active"] = after(
            (jax.nn.silu(gate_val.astype(F32)) * up_val.astype(F32)).astype(BF16)
        )
    for micro in micros[1:]:
        state[micro]["branch"] = gather_branch(micro, state[0]["hidden"], state[0]["active"])

    def both(name):
        return [st[name] for st in state]

    down_part = weight_grad(both("branch"), both("active"))
    down_grad = scatter_dp(down_part)

    for micro in micros:
        st = state[micro]
        gate_val, up_val = st["gate"].astype(F32), st["up"].astype(F32)
        sigmoid_gate = jax.nn.sigmoid(gate_val)
        grad_active = dot(st["branch"], down_t, 1, 0)
        grad_gate = (
            grad_active * up_val * sigmoid_gate * (1.0 + gate_val * (1.0 - sigmoid_gate))
        ).astype(BF16)
        grad_up = (grad_active * gate_val * sigmoid_gate).astype(BF16)
        grad_gate, grad_up = after((grad_gate, grad_up), down_part)
        st["grad_gate"], st["grad_up"] = grad_gate, grad_up
        grad_hidden = scatter_ring(
            lambda names, half: dot(
                ring_rows(grad_gate, names, rows), half_rows(proj_gate, half), 1, 1
            )
            + dot(ring_rows(grad_up, names, rows), half_rows(proj_up, half), 1, 1)
        )
        grad_mid_norm, st["post_gain_grad"] = norm_back(st["middle"], gain_post, grad_hidden)
        st["grad_mid"] = cotangent[micro].astype(F32) + grad_mid_norm
        st["attn_grad"] = true_order((RESIDUAL * st["grad_mid"]).astype(BF16))
    gate_part = weight_grad(both("hidden"), both("grad_gate"))
    gate_grad = scatter_dp(after(gate_part, down_grad))
    up_part = weight_grad(both("hidden"), both("grad_up"))
    up_grad = scatter_dp(after(up_part, gate_grad))

    for micro in micros:
        st = state[micro]
        attn_grad = after(st["attn_grad"], gate_part, up_part)
        grad_t = dot(out_t, attn_grad, 0, 1).astype(BF16).reshape(heads, VD, seq_length)
        dquery_t, dkeyval_t, drope_t = attend_back(
            prefix[micro],
            st["queries_t"],
            st["keyval_t"],
            st["rope_t"],
            grad_t,
            st["logs"],
            cos_t,
            sin_t,
            *([] if micro else [gate_grad]),
        )
        st["dquery_t"] = dquery_t.reshape(heads * HEAD, seq_length)
        st["dkeyval_t"] = dkeyval_t.reshape(heads * (NOPE + VD), seq_length)
        comp_part = dot(st["dquery_t"], up_query, 0, 1)
        norm_part = dot(st["dkeyval_t"], up_latent, 0, 1)
        latent_part = jnp.concatenate(
            [comp_part.astype(BF16), norm_part.astype(BF16), drope_t.T.astype(BF16)], axis=1
        )
        st["grad_lat"] = scatter_ring(
            lambda names, half: true_rows(half_columns(latent_part, half), names, 0).astype(F32)
        )

    out_part = add_micros(lambda st: dot(st["attn_grad"], st["attended_t"], 0, 1))
    out_grad = scatter_dp(after(out_part, up_grad))
    query_up_part = add_micros(lambda st: dot(st["query_full"], st["dquery_t"], 0, 1))
    latent_up_part = add_micros(lambda st: dot(st["latent_full"], st["dkeyval_t"], 0, 1))
    ups_part = jnp.concatenate(
        [
            widen(query_up_part, latent_columns).reshape(dp_size, query_rows, latent_columns),
            latent_up_part.reshape(dp_size, latent_rows, latent_columns),
        ],
        axis=1,
    ).reshape(-1, latent_columns)
    ups_grad = scatter_dp(after(ups_part, out_grad))

    grad_lat = jnp.concatenate([st["grad_lat"] for st in state], axis=0)
    grad_qlat, query_gain_grad = norm_back(query_lat, gain_query, grad_lat[:, :query_rank])
    grad_comp, latent_gain_grad = norm_back(
        latent_comp, gain_latent, grad_lat[:, query_rank : query_rank + KVR]
    )
    grad_rope = rotate(grad_lat[:, query_rank + KVR :], cos_both, -sin_both)
    grad_down = widen(
        jnp.concatenate(
            [grad_qlat.astype(BF16), grad_comp.astype(BF16), grad_rope.astype(BF16)], axis=1
        ),
        packed_width,
    )
    grad_normed = dot(grad_down, packed, 1, 1)
    grad_resid, input_gain_grad = norm_back(residual, gain_in, grad_normed)
    small_grad = jnp.concatenate(
        [
            query_gain_grad.reshape(devices, query_own),
            latent_gain_grad.reshape(devices, latent_own),
            jnp.zeros((devices, own_rows - query_own - latent_own), F32),
        ],
        axis=1,
    ).reshape(width)
    post_gain_grad = sum(st["post_gain_grad"] for st in state)
    vectors = jnp.stack([input_gain_grad, post_gain_grad, small_grad], axis=1)
    vectors = jnp.pad(vectors, ((0, 0), (down_rank, packed_width - down_rank - 3)))
    packed_grad = scatter_everywhere(
        (dot(normed, grad_down, 0, 0) + vectors).astype(BF16), (ups_grad,)
    )
    packed_grad = packed_grad.astype(F32)
    d_tokens = [
        st["grad_mid"] + of_micro(grad_resid, micro) for micro, st in enumerate(state)
    ]

    mixed = []
    for micro in micros:
        st = state[micro]
        active = after(st["active"], state[-1]["attn_grad"])
        mlp_rows = scatter_ring(
            lambda names, half: dot(
                ring_rows(active, names, rows), half_rows(down_t, half), 1, 1
            )
        )
        mixed.append((st["middle"] + RESIDUAL * mlp_rows).astype(BF16))

    small_grad = packed_grad[:, down_rank + 2]
    return (
        jnp.stack(mixed, axis=0),
        jnp.stack(d_tokens, axis=0),
        packed_grad[:, down_rank],
        packed_grad[:, :query_rank],
        small_grad[:query_own],
        ups_grad[:query_rows, :query_columns].astype(F32),
        packed_grad[:, query_rank:down_rank],
        small_grad[query_own : query_own + latent_own],
        ups_grad[query_rows:].astype(F32),
        out_grad.T.astype(F32),
        packed_grad[:, down_rank + 1],
        gate_grad.astype(F32),
        up_grad.astype(F32),
        down_grad.T.astype(F32),
    )


def solution(mesh):
    dp_size, tensor_size = mesh.devices.shape
    mesh = Mesh(mesh.devices.reshape(dp_size // 2, 2, tensor_size), EVERYWHERE)
    return jax.shard_map(
        body,
        mesh=mesh,
        in_specs=(
            P(None, EVERYWHERE, None),
            P(None, DP),
            P(EVERYWHERE),
            P(EVERYWHERE, None),
            P(EVERYWHERE),
            P(DP, "tensor"),
            P(EVERYWHERE, None),
            P(EVERYWHERE),
            P(DP, "tensor"),
            P("tensor", DP),
            P(EVERYWHERE),
            P(DP, "tensor"),
            P(DP, "tensor"),
            P("tensor", DP),
            P(None, EVERYWHERE, None),
        ),
        out_specs=(
            P(None, EVERYWHERE, None),
            P(None, EVERYWHERE, None),
            P(EVERYWHERE),
            P(EVERYWHERE, None),
            P(EVERYWHERE),
            P(DP, "tensor"),
            P(EVERYWHERE, None),
            P(EVERYWHERE),
            P(DP, "tensor"),
            P("tensor", DP),
            P(EVERYWHERE),
            P(DP, "tensor"),
            P(DP, "tensor"),
            P("tensor", DP),
        ),
        check_vma=False,
    )
```

```python
import functools
import math

import jax
import jax.numpy as jnp
from jax import lax
from jax.experimental import pallas as pl
from jax.experimental.pallas import tpu as pltpu
from jax.sharding import Mesh
from jax.sharding import PartitionSpec as P

NOPE = 64
ROPE = 32
VD = 64
KVR = 256
HEAD = NOPE + ROPE
PREFIX_MAX = 512
BLOCK = 256

DP = ("ring", "core")
EVERYWHERE = ("ring", "core", "tensor")

EPSILON = 1e-05
RESIDUAL = 1.4 / math.sqrt(62.0)
NEGATIVE = -1e30
ROPE_BASE = 10000.0
SCALE = HEAD ** (-0.5)

BF16 = jnp.bfloat16
F32 = jnp.float32


def dot(left_side, right_side, left_dim, right_dim):
    return lax.dot_general(
        left_side, right_side, (((left_dim,), (right_dim,)), ((), ())), preferred_element_type=F32
    )


def inverse_rms(values):
    return lax.rsqrt(jnp.mean(values * values, axis=-1, keepdims=True) + EPSILON)


def norm_back(values, gain_vec, grad_out):
    scale_inv = inverse_rms(values)
    normal = values * scale_inv
    grad_norm = grad_out * gain_vec
    grad_values = scale_inv * (
        grad_norm - normal * jnp.mean(grad_norm * normal, axis=-1, keepdims=True)
    )
    return (grad_values, jnp.sum(grad_out * normal, axis=0))


def rotary(row_count, row_start):
    half_width = ROPE // 2
    frequency = ROPE_BASE ** (-2.0 * jnp.arange(half_width).astype(F32) / ROPE)
    angles = (row_start + jnp.arange(row_count)).astype(F32)[:, None] * frequency[None, :]
    return (jnp.cos(angles), jnp.sin(angles))


def rotate(values, cosine, sine_table, axis=-1):
    first_half, second_half = jnp.split(values, 2, axis=axis)
    return jnp.concatenate(
        [
            first_half * cosine - second_half * sine_table,
            second_half * cosine + first_half * sine_table,
        ],
        axis=axis,
    )


def key_width(block_index, seq_length):
    return min(max((block_index + 1) * BLOCK, PREFIX_MAX), seq_length)


def block_scores(keys, query_block, block_index, width, prefix_len):
    scores = jnp.dot(keys[:width], query_block, preferred_element_type=F32)
    first = block_index * BLOCK
    tail = scores[first:]
    key_at = first + lax.broadcasted_iota(jnp.int32, tail.shape, 0)
    query_at = first + lax.broadcasted_iota(jnp.int32, tail.shape, 1)
    tail = jnp.where((key_at <= query_at) | (key_at < prefix_len), tail, NEGATIVE)
    if first:
        return jnp.concatenate([scores[:first], tail], axis=0)
    return tail


def attend_kernel(prefix_ref, query_ref, keyval_ref, rope_ref, out_ref, log_ref):
    seq_length = query_ref.shape[-1]
    prefix_len = prefix_ref[0]
    keyval = keyval_ref[0]
    keys = jnp.concatenate([keyval[:NOPE], rope_ref[...]], axis=0).T
    values_t = keyval[NOPE:]
    for block_index in range(seq_length // BLOCK):
        at = pl.ds(block_index * BLOCK, BLOCK)
        width = key_width(block_index, seq_length)
        scores = block_scores(keys, query_ref[0, :, at], block_index, width, prefix_len)
        peak = jnp.max(scores, axis=0, keepdims=True)
        exp_scores = jnp.exp((scores - peak) * SCALE)
        total = jnp.sum(exp_scores, axis=0, keepdims=True)
        block_out = jnp.dot(
            values_t[:, :width], exp_scores.astype(BF16), preferred_element_type=F32
        )
        out_ref[0, :, at] = (block_out / total).astype(BF16)
        log_ref[0, :, at] = peak * SCALE + jnp.log(total)


def attend(prefix_len, queries_t, keyval_t, rope_t):
    heads, _, seq_length = queries_t.shape
    head_block = lambda rows: pl.BlockSpec((1, rows, seq_length), lambda h: (h, 0, 0))
    return pl.pallas_call(
        attend_kernel,
        grid=(heads,),
        in_specs=[
            pl.BlockSpec(memory_space=pltpu.SMEM),
            head_block(HEAD),
            head_block(NOPE + VD),
            pl.BlockSpec((ROPE, seq_length), lambda h: (0, 0)),
        ],
        out_specs=[head_block(VD), head_block(1)],
        out_shape=[
            jax.ShapeDtypeStruct((heads, VD, seq_length), BF16),
            jax.ShapeDtypeStruct((heads, 1, seq_length), F32),
        ],
        compiler_params=pltpu.CompilerParams(vmem_limit_bytes=40 * 2**20),
        cost_estimate=pl.CostEstimate(
            flops=2 * heads * seq_length * seq_length * 384,
            bytes_accessed=heads * seq_length * 600,
            transcendentals=heads * seq_length * seq_length,
        ),
        name="attend",
    )(prefix_len, queries_t, keyval_t, rope_t)


def attend_back_kernel(
    prefix_ref,
    query_ref,
    keyval_ref,
    rope_ref,
    grad_ref,
    log_ref,
    cos_ref,
    sin_ref,
    *refs,
):
    dquery_ref, dkeyval_ref, drope_ref, dkey_acc, dvalue_acc = refs[-5:]
    seq_length = query_ref.shape[-1]
    prefix_len = prefix_ref[0]
    keyval = keyval_ref[0]
    keys_t = jnp.concatenate([keyval[:NOPE], rope_ref[...]], axis=0)
    keys = keys_t.T
    values = keyval[NOPE:].T
    dkey_acc[...] = jnp.zeros_like(dkey_acc)
    dvalue_acc[...] = jnp.zeros_like(dvalue_acc)
    for block_index in range(seq_length // BLOCK):
        at = pl.ds(block_index * BLOCK, BLOCK)
        width = key_width(block_index, seq_length)
        query_block = query_ref[0, :, at]
        grad_block = grad_ref[0, :, at]
        scores = block_scores(keys, query_block, block_index, width, prefix_len)
        soft = jnp.exp(scores * SCALE - log_ref[0, :, at])
        grad_probs = jnp.dot(values[:width], grad_block, preferred_element_type=F32)
        delta = jnp.sum(soft * grad_probs, axis=0, keepdims=True)
        grad_scores = (soft * (grad_probs - delta)).astype(BF16)
        dquery = SCALE * jnp.dot(keys_t[:, :width], grad_scores, preferred_element_type=F32)
        dquery_ref[0, :NOPE, at] = dquery[:NOPE].astype(BF16)
        dquery_ref[0, NOPE:, at] = rotate(
            dquery[NOPE:], cos_ref[:, at], -sin_ref[:, at], axis=0
        ).astype(BF16)
        dkey_acc[:, :width] += dot(query_block, grad_scores, 1, 1)
        dvalue_acc[:, :width] += dot(grad_block, soft.astype(BF16), 1, 1)
    dkeyval_ref[0, :NOPE, :] = (SCALE * dkey_acc[:NOPE, :]).astype(BF16)
    dkeyval_ref[0, NOPE:, :] = dvalue_acc[...].astype(BF16)
    rope_part = SCALE * dkey_acc[NOPE:, :]

    @pl.when(pl.program_id(0) == 0)
    def _():
        drope_ref[...] = rope_part

    @pl.when(pl.program_id(0) > 0)
    def _():
        drope_ref[...] += rope_part


def attend_back(prefix_len, queries_t, keyval_t, rope_t, grad_t, logs, cos_t, sin_t, *others):
    heads, _, seq_length = queries_t.shape
    head_block = lambda rows: pl.BlockSpec((1, rows, seq_length), lambda h: (h, 0, 0))
    whole = lambda rows: pl.BlockSpec((rows, seq_length), lambda h: (0, 0))
    return pl.pallas_call(
        attend_back_kernel,
        grid=(heads,),
        in_specs=[
            pl.BlockSpec(memory_space=pltpu.SMEM),
            head_block(HEAD),
            head_block(NOPE + VD),
            whole(ROPE),
            head_block(VD),
            head_block(1),
            whole(ROPE // 2),
            whole(ROPE // 2),
            *[pl.BlockSpec(memory_space=pl.ANY) for other in others],
        ],
        out_specs=[head_block(HEAD), head_block(NOPE + VD), whole(ROPE)],
        out_shape=[
            jax.ShapeDtypeStruct((heads, HEAD, seq_length), BF16),
            jax.ShapeDtypeStruct((heads, NOPE + VD, seq_length), BF16),
            jax.ShapeDtypeStruct((ROPE, seq_length), F32),
        ],
        scratch_shapes=[
            pltpu.VMEM((HEAD, seq_length), F32),
            pltpu.VMEM((VD, seq_length), F32),
        ],
        compiler_params=pltpu.CompilerParams(vmem_limit_bytes=40 * 2**20),
        cost_estimate=pl.CostEstimate(
            flops=2 * heads * seq_length * seq_length * 960,
            bytes_accessed=heads * seq_length * 1100,
            transcendentals=heads * seq_length * seq_length,
        ),
        name="attend_back",
    )(prefix_len, queries_t, keyval_t, rope_t, grad_t, logs, cos_t, sin_t, *others)


def weight_grad_kernel(*refs):
    out_ref = refs[-1]
    pairs = len(refs) // 2
    total = None
    for left_ref, right_ref in zip(refs[:pairs], refs[pairs:]):
        term = dot(left_ref[...], right_ref[...], 0, 0)
        total = term if total is None else total + term
    out_ref[...] = total.astype(BF16)


def weight_grad(lefts, rights):
    tokens, rows = lefts[0].shape
    columns = rights[0].shape[1]
    tile = 512 if rows % 512 == 0 else rows
    return pl.pallas_call(
        weight_grad_kernel,
        grid=(rows // tile,),
        in_specs=[pl.BlockSpec((tokens, tile), lambda i: (0, i))] * len(lefts)
        + [pl.BlockSpec((tokens, columns), lambda i: (0, 0))] * len(rights),
        out_specs=pl.BlockSpec((tile, columns), lambda i: (i, 0)),
        out_shape=jax.ShapeDtypeStruct((rows, columns), BF16),
        compiler_params=pltpu.CompilerParams(vmem_limit_bytes=56 * 2**20),
        cost_estimate=pl.CostEstimate(
            flops=2 * len(lefts) * tokens * rows * columns,
            bytes_accessed=2 * (len(lefts) * tokens * (rows + columns) + rows * columns),
            transcendentals=0,
        ),
        name="weight_grad",
    )(*lefts, *rights)


def swap(values, bit):
    return lax.ppermute(values, "tensor", [(index, index ^ bit) for index in range(4)])


def gather_blocks(values, hold=()):
    half = values.shape[0] // 2
    from_x = swap(values, 1)
    from_y = swap(values, 2)
    if hold:
        from_x, from_y = after((from_x, from_y), *hold)
    far_top = swap(from_y[:half], 1)
    far_low = swap(from_x[half:], 2)
    return (values, from_x, far_top, far_low, from_y)


def two_by_two():
    return lax.axis_size("tensor") == 4


def gather_ring(values, hold=()):
    if not two_by_two():
        return lax.all_gather(values, "tensor", axis=0, tiled=True)
    return jnp.concatenate(gather_blocks(values, hold), axis=0)


def scatter_ring(part):
    if not two_by_two():
        total = part("all", None).astype(BF16)
        return lax.psum_scatter(total, "tensor", scatter_dimension=0, tiled=True).astype(F32)
    rx = swap(part("xd", 0).astype(BF16), 1)
    ry = swap(part("dy", 1).astype(BF16), 2)
    rows = rx.shape[0] // 2
    to_y = (part("y", 0) + rx[rows:].astype(F32)).astype(BF16)
    to_x = (part("x", 1) + ry[:rows].astype(F32)).astype(BF16)
    ry2 = swap(to_y, 2)
    rx2 = swap(to_x, 1)
    left = part("o", 0) + rx[:rows].astype(F32) + ry2.astype(F32)
    right = part("o", 1) + ry[rows:].astype(F32) + rx2.astype(F32)
    return jnp.concatenate([left, right], axis=-1)


RING = {"o": (0, 1), "x": (1, 1), "xd": (1, 2), "dy": (2, 2), "y": (3, 1)}
FLIP = {"o": 0, "x": 1, "d": 3, "y": 2}


def ring_rows(values, names, rows):
    if names == "all":
        return values
    start, count = RING[names]
    return values[start * rows : (start + count) * rows]


def half_rows(weight, half):
    if half is None:
        return weight
    size = weight.shape[0] // 2
    return weight[half * size : (half + 1) * size]


def half_columns(values, half):
    if half is None:
        return values
    split = round(values.shape[1] / 256) * 128
    return values[:, split:] if half else values[:, :split]


def after(values, *others):
    return lax.optimization_barrier((values, *others))[0]


def nothing_kernel(*refs):
    pass


def tie(values, *others):
    if not others:
        return values
    anywhere = pl.BlockSpec(memory_space=pl.ANY)
    return pl.pallas_call(
        nothing_kernel,
        in_specs=[anywhere] * (1 + len(others)),
        out_specs=anywhere,
        out_shape=jax.ShapeDtypeStruct(values.shape, values.dtype),
        input_output_aliases={0: 0},
        name="tie",
    )(values, *others)


def widen(values, columns):
    return jnp.pad(values, ((0, 0), (0, columns - values.shape[1])))


def swap_cores(values):
    return lax.ppermute(values, "core", [(0, 1), (1, 0)])


def gather_everywhere(values):
    if not two_by_two():
        return lax.all_gather(values, EVERYWHERE, axis=0, tiled=True)
    rows, columns = values.shape
    own = lax.all_gather(values, DP, axis=0, tiled=True)
    size = own.shape[0] // 2
    core = lax.axis_index("core")
    tensor_at = lax.axis_index("tensor")
    mine = gather_ring(lax.dynamic_slice_in_dim(own, core * size, size, 0))
    other = swap_cores(mine)
    result = jnp.zeros((2, size // rows, 4, rows, columns), values.dtype)
    for side, pieces in ((core, mine), (1 - core, other)):
        for index, bit in enumerate((0, 1, 3, 2)):
            piece = pieces[index * size : (index + 1) * size]
            result = lax.dynamic_update_slice(
                result,
                piece.reshape(1, size // rows, 1, rows, columns),
                (side, 0, tensor_at ^ bit, 0, 0),
            )
    return result.reshape(-1, columns)


def scatter_everywhere(values, last_after):
    if not two_by_two():
        return lax.psum_scatter(values, EVERYWHERE, scatter_dimension=0, tiled=True)
    columns = values.shape[1]
    ring = lax.axis_size("ring")
    rows = values.shape[0] // (ring * 8)
    core = lax.axis_index("core")
    tensor_at = lax.axis_index("tensor")
    blocks = values.reshape(ring, 2, 4, rows, columns)
    pick = lambda index: lax.dynamic_slice_in_dim(blocks, index, 1, 1)[:, 0]
    chip = pick(core).astype(F32) + swap_cores(pick(1 - core)).astype(F32)
    chip = chip.astype(BF16)

    def part(names, half):
        pieces = [
            lax.dynamic_slice_in_dim(chip, tensor_at ^ FLIP[name], 1, 1).reshape(-1, columns)
            for name in names
        ]
        return half_columns(jnp.concatenate(pieces, axis=0), half).astype(F32)

    mine = after(scatter_ring(part).astype(BF16), *last_after)
    return lax.psum_scatter(mine, "ring", scatter_dimension=0, tiled=True)


def body(
    tokens,
    prefix,
    input_gain,
    query_down,
    query_gain,
    query_up,
    latent_down,
    latent_gain,
    latent_up,
    out_proj,
    post_gain,
    gate_proj,
    up_proj,
    down_proj,
    cotangent,
):
    micros = range(tokens.shape[0])
    rows = tokens.shape[1]
    width = tokens.shape[2]
    tensor_at = lax.axis_index("tensor")
    devices = lax.axis_size(EVERYWHERE)
    dp_size = lax.axis_size(DP)
    seq_length = rows * lax.axis_size("tensor")
    query_rank = query_down.shape[1]
    latent_rank = latent_down.shape[1]
    down_rank = query_rank + latent_rank
    packed_width = -(-(down_rank + 3) // 128) * 128
    own_rows = input_gain.shape[0]
    query_own = query_gain.shape[0]
    latent_own = latent_gain.shape[0]

    def gather_dp(values):
        return lax.all_gather(values, DP, axis=0, tiled=True)

    def scatter_dp(values):
        return lax.psum_scatter(values, DP, scatter_dimension=0, tiled=True)

    small = jnp.zeros((own_rows,), BF16)
    small = small.at[:query_own].set(query_gain)
    small = small.at[query_own : query_own + latent_own].set(latent_gain)
    packed = gather_everywhere(
        widen(
            jnp.concatenate(
                [query_down, latent_down, input_gain[:, None], post_gain[:, None], small[:, None]],
                axis=1,
            ),
            packed_width,
        )
    )
    query_rows, query_columns = query_up.shape
    latent_rows, latent_columns = latent_up.shape
    ups = gather_dp(jnp.concatenate([widen(query_up, latent_columns), latent_up], axis=0))
    ups = ups.reshape(dp_size, query_rows + latent_rows, latent_columns)
    up_query = ups[:, :query_rows, :query_columns].reshape(-1, query_columns)
    up_latent = ups[:, query_rows:].reshape(-1, latent_columns)
    out_t = gather_dp(out_proj.T)
    proj_gate = gather_dp(gate_proj)
    proj_up = gather_dp(up_proj)
    down_t = gather_dp(down_proj.T)

    gains = packed[:, down_rank : down_rank + 3].astype(F32)
    gain_in = gains[:, 0]
    gain_post = gains[:, 1]
    small_all = gains[:, 2].reshape(devices, own_rows)
    gain_query = small_all[:, :query_own].reshape(query_rank)
    gain_latent = small_all[:, query_own : query_own + latent_own].reshape(KVR)

    first_row = tensor_at * rows
    cos_local, sin_local = rotary(rows, first_row)
    cos_all, sin_all = rotary(seq_length, 0)
    cos_t, sin_t = cos_all.T, sin_all.T
    heads = up_query.shape[1] // HEAD

    def true_order(values):
        if not two_by_two():
            return lax.all_gather(values, "tensor", axis=0, tiled=True)
        own, from_x, far_top, far_low, from_y = gather_blocks(values)
        far = jnp.concatenate([far_top, far_low], axis=0)
        result = jnp.zeros((seq_length, values.shape[1]), values.dtype)
        for bit, piece in ((0, own), (1, from_x), (2, from_y), (3, far)):
            result = lax.dynamic_update_slice(result, piece, ((tensor_at ^ bit) * rows, 0))
        return result

    def true_block(values, name, axis):
        return lax.dynamic_slice_in_dim(values, (tensor_at ^ FLIP[name]) * rows, rows, axis)

    def true_rows(values, names, axis):
        if names == "all":
            return values
        pieces = [true_block(values, name, axis) for name in names]
        return pieces[0] if len(pieces) == 1 else jnp.concatenate(pieces, axis=axis)

    residual = tokens.reshape(-1, width).astype(F32)
    normed = (residual * inverse_rms(residual) * gain_in).astype(BF16)
    lat = dot(normed, packed, 1, 0)
    query_lat = lat[:, :query_rank]
    latent_comp = lat[:, query_rank : query_rank + KVR]
    query_comp = (query_lat * inverse_rms(query_lat) * gain_query).astype(BF16)
    latent_norm = (latent_comp * inverse_rms(latent_comp) * gain_latent).astype(BF16)
    cos_both = jnp.concatenate([cos_local for micro in micros], axis=0)
    sin_both = jnp.concatenate([sin_local for micro in micros], axis=0)
    key_rope = rotate(lat[:, query_rank + KVR : down_rank], cos_both, sin_both).astype(BF16)
    latents = jnp.concatenate([query_comp, latent_norm, key_rope], axis=1)

    def of_micro(values, micro):
        return values[micro * rows : (micro + 1) * rows]

    state = []
    for micro in micros:
        full = true_order(of_micro(latents, micro))
        state.append(
            dict(
                query_full=full[:, :query_rank],
                latent_full=full[:, query_rank : query_rank + KVR],
                rope_t=full[:, query_rank + KVR :].T,
            )
        )

    def gather_branch(micro, start_after, hold):
        branch = (RESIDUAL * cotangent[micro].astype(F32)).astype(BF16)
        return gather_ring(tie(branch, start_after), (hold,))

    for micro in micros:
        st = state[micro]
        raw_t = dot(up_query, st["query_full"], 0, 1).reshape(heads, HEAD, seq_length)
        st["queries_t"] = jnp.concatenate(
            [raw_t[:, :NOPE], rotate(raw_t[:, NOPE:], cos_t[None], sin_t[None], axis=1)], axis=1
        ).astype(BF16)
        st["keyval_t"] = (
            dot(up_latent, st["latent_full"], 0, 1)
            .astype(BF16)
            .reshape(heads, NOPE + VD, seq_length)
        )
        attended_t, st["logs"] = attend(
            prefix[micro], st["queries_t"], st["keyval_t"], st["rope_t"]
        )
        st["attended_t"] = attended_t.reshape(heads * VD, seq_length)
        attn_rows = scatter_ring(
            lambda names, half: dot(
                true_rows(st["attended_t"], names, 1), half_rows(out_t, half), 0, 1
            )
        )
        st["middle"] = tokens[micro].astype(F32) + RESIDUAL * attn_rows
        hidden_in = (st["middle"] * inverse_rms(st["middle"]) * gain_post).astype(BF16)
        st["hidden"] = gather_ring(hidden_in)

    state[0]["branch"] = gather_branch(0, state[1]["query_full"], state[0]["attended_t"])

    def add_micros(term):
        total = term(state[0])
        for micro in micros[1:]:
            total = total + term(state[micro])
        return total.astype(BF16)

    state[0]["hidden"] = after(state[0]["hidden"], *[st["attended_t"] for st in state[1:]])
    for micro in micros:
        st = state[micro]
        gate_val = dot(st["hidden"], proj_gate, 1, 0).astype(BF16)
        up_val = dot(st["hidden"], proj_up, 1, 0).astype(BF16)
        gate_val, up_val = lax.optimization_barrier((gate_val, up_val))
        st["gate"], st["up"] = gate_val, up_val
        st["active"] = after(
            (jax.nn.silu(gate_val.astype(F32)) * up_val.astype(F32)).astype(BF16)
        )
    for micro in micros[1:]:
        state[micro]["branch"] = gather_branch(micro, state[0]["hidden"], state[0]["active"])

    def both(name):
        return [st[name] for st in state]

    down_part = weight_grad(both("branch"), both("active"))
    down_grad = scatter_dp(down_part)

    for micro in micros:
        st = state[micro]
        gate_val, up_val = st["gate"].astype(F32), st["up"].astype(F32)
        sigmoid_gate = jax.nn.sigmoid(gate_val)
        grad_active = dot(st["branch"], down_t, 1, 0)
        grad_gate = (
            grad_active * up_val * sigmoid_gate * (1.0 + gate_val * (1.0 - sigmoid_gate))
        ).astype(BF16)
        grad_up = (grad_active * gate_val * sigmoid_gate).astype(BF16)
        grad_gate, grad_up = after((grad_gate, grad_up), down_part)
        st["grad_gate"], st["grad_up"] = grad_gate, grad_up
        grad_hidden = scatter_ring(
            lambda names, half: dot(
                ring_rows(grad_gate, names, rows), half_rows(proj_gate, half), 1, 1
            )
            + dot(ring_rows(grad_up, names, rows), half_rows(proj_up, half), 1, 1)
        )
        grad_mid_norm, st["post_gain_grad"] = norm_back(st["middle"], gain_post, grad_hidden)
        st["grad_mid"] = cotangent[micro].astype(F32) + grad_mid_norm
        st["attn_grad"] = true_order((RESIDUAL * st["grad_mid"]).astype(BF16))
    gate_part = weight_grad(both("hidden"), both("grad_gate"))
    gate_grad = scatter_dp(after(gate_part, down_grad))
    up_part = weight_grad(both("hidden"), both("grad_up"))
    up_grad = scatter_dp(up_part)

    for micro in micros:
        st = state[micro]
        attn_grad = after(st["attn_grad"], gate_part, up_part)
        grad_t = dot(out_t, attn_grad, 0, 1).astype(BF16).reshape(heads, VD, seq_length)
        dquery_t, dkeyval_t, drope_t = attend_back(
            prefix[micro],
            st["queries_t"],
            st["keyval_t"],
            st["rope_t"],
            grad_t,
            st["logs"],
            cos_t,
            sin_t,
            *([] if micro else [gate_grad]),
        )
        st["dquery_t"] = dquery_t.reshape(heads * HEAD, seq_length)
        st["dkeyval_t"] = dkeyval_t.reshape(heads * (NOPE + VD), seq_length)
        comp_part = dot(st["dquery_t"], up_query, 0, 1)
        norm_part = dot(st["dkeyval_t"], up_latent, 0, 1)
        latent_part = jnp.concatenate(
            [comp_part.astype(BF16), norm_part.astype(BF16), drope_t.T.astype(BF16)], axis=1
        )
        st["grad_lat"] = scatter_ring(
            lambda names, half: true_rows(half_columns(latent_part, half), names, 0).astype(F32)
        )

    out_part = add_micros(lambda st: dot(st["attn_grad"], st["attended_t"], 0, 1))
    out_grad = scatter_dp(after(out_part, up_grad))
    query_up_part = add_micros(lambda st: dot(st["query_full"], st["dquery_t"], 0, 1))
    latent_up_part = add_micros(lambda st: dot(st["latent_full"], st["dkeyval_t"], 0, 1))
    ups_part = jnp.concatenate(
        [
            widen(query_up_part, latent_columns).reshape(dp_size, query_rows, latent_columns),
            latent_up_part.reshape(dp_size, latent_rows, latent_columns),
        ],
        axis=1,
    ).reshape(-1, latent_columns)
    ups_grad = scatter_dp(after(ups_part, out_grad))

    grad_lat = jnp.concatenate([st["grad_lat"] for st in state], axis=0)
    grad_qlat, query_gain_grad = norm_back(query_lat, gain_query, grad_lat[:, :query_rank])
    grad_comp, latent_gain_grad = norm_back(
        latent_comp, gain_latent, grad_lat[:, query_rank : query_rank + KVR]
    )
    grad_rope = rotate(grad_lat[:, query_rank + KVR :], cos_both, -sin_both)
    grad_down = widen(
        jnp.concatenate(
            [grad_qlat.astype(BF16), grad_comp.astype(BF16), grad_rope.astype(BF16)], axis=1
        ),
        packed_width,
    )
    grad_normed = dot(grad_down, packed, 1, 1)
    grad_resid, input_gain_grad = norm_back(residual, gain_in, grad_normed)
    small_grad = jnp.concatenate(
        [
            query_gain_grad.reshape(devices, query_own),
            latent_gain_grad.reshape(devices, latent_own),
            jnp.zeros((devices, own_rows - query_own - latent_own), F32),
        ],
        axis=1,
    ).reshape(width)
    post_gain_grad = sum(st["post_gain_grad"] for st in state)
    vectors = jnp.stack([input_gain_grad, post_gain_grad, small_grad], axis=1)
    vectors = jnp.pad(vectors, ((0, 0), (down_rank, packed_width - down_rank - 3)))
    packed_grad = scatter_everywhere(
        (dot(normed, grad_down, 0, 0) + vectors).astype(BF16), (ups_grad,)
    )
    packed_grad = packed_grad.astype(F32)
    d_tokens = [
        st["grad_mid"] + of_micro(grad_resid, micro) for micro, st in enumerate(state)
    ]

    mixed = []
    for micro in micros:
        st = state[micro]
        active = after(st["active"], state[-1]["attn_grad"])
        mlp_rows = scatter_ring(
            lambda names, half: dot(
                ring_rows(active, names, rows), half_rows(down_t, half), 1, 1
            )
        )
        mixed.append((st["middle"] + RESIDUAL * mlp_rows).astype(BF16))

    small_grad = packed_grad[:, down_rank + 2]
    return (
        jnp.stack(mixed, axis=0),
        jnp.stack(d_tokens, axis=0),
        packed_grad[:, down_rank],
        packed_grad[:, :query_rank],
        small_grad[:query_own],
        ups_grad[:query_rows, :query_columns].astype(F32),
        packed_grad[:, query_rank:down_rank],
        small_grad[query_own : query_own + latent_own],
        ups_grad[query_rows:].astype(F32),
        out_grad.T.astype(F32),
        packed_grad[:, down_rank + 1],
        gate_grad.astype(F32),
        up_grad.astype(F32),
        down_grad.T.astype(F32),
    )


def solution(mesh):
    dp_size, tensor_size = mesh.devices.shape
    mesh = Mesh(mesh.devices.reshape(dp_size // 2, 2, tensor_size), EVERYWHERE)
    return jax.shard_map(
        body,
        mesh=mesh,
        in_specs=(
            P(None, EVERYWHERE, None),
            P(None, DP),
            P(EVERYWHERE),
            P(EVERYWHERE, None),
            P(EVERYWHERE),
            P(DP, "tensor"),
            P(EVERYWHERE, None),
            P(EVERYWHERE),
            P(DP, "tensor"),
            P("tensor", DP),
            P(EVERYWHERE),
            P(DP, "tensor"),
            P(DP, "tensor"),
            P("tensor", DP),
            P(None, EVERYWHERE, None),
        ),
        out_specs=(
            P(None, EVERYWHERE, None),
            P(None, EVERYWHERE, None),
            P(EVERYWHERE),
            P(EVERYWHERE, None),
            P(EVERYWHERE),
            P(DP, "tensor"),
            P(EVERYWHERE, None),
            P(EVERYWHERE),
            P(DP, "tensor"),
            P("tensor", DP),
            P(EVERYWHERE),
            P(DP, "tensor"),
            P(DP, "tensor"),
            P("tensor", DP),
        ),
        check_vma=False,
    )
```
